32 devices in a mesh: groups: 2 (over y), inst: 4 (over z), section: 2 (over x), tp: 2 (over core).
Axes of the slice: x: 2, y: 2, z: 4, core: 2. Of those that a mesh axis runs over, the one named last changes fastest.
Arguments:
- emb: bfloat16 [4, 32, 8192], P(None, ('groups', 'inst'), 'tp'), parts along dimension 1, may hold values from -24 to 24
- attn_gain: float32 [2, 8192], P('section', 'tp'), may hold values from 0.1 to 1.9
- out_gain: float32 [2, 8192], P('section', 'tp'), may hold values from 0.4 to 1.6
- k_cache: bfloat16 [8, 2, 24, 128, 1024], P(('groups', 'inst'), 'section', None, None, 'tp'), parts along dimension 0, may hold values from -128 to 128
- v_cache: bfloat16 [8, 2, 24, 128, 1024], P(('groups', 'inst'), 'section', None, None, 'tp'), parts along dimension 0, may hold values from -6 to 6
- tables: int32 [8, 4, 6], P(('groups', 'inst')), parts along dimension 0, may hold values from 0 to 23, as said below
- lens: int32 [8, 4], P('groups'), parts along dimension 0, may hold values from 2 to 764
- partner: int32 [4], replicated, may hold values from 0 to 3, as said below
- mig_req: int32 [8], P('groups'), parts along dimension 0, may hold values from 0 to 3
Outputs:
- layer_out: bfloat16 [2, 4, 32, 8192], P('section', None, ('groups', 'inst'), 'tp'), parts along dimension 2
- arrived_k: bfloat16 [8, 2, 768, 1024], P(('groups', 'inst'), 'section', None, 'tp'), parts along dimension 0
- arrived_v: bfloat16 [8, 2, 768, 1024], P(('groups', 'inst'), 'section', None, 'tp'), parts along dimension 0
The draws below stay inside these ranges and needn't reach their ends.
There are 2 independent parts, one for each index of `groups`. The reference program is written for one: setup_inputs(seed, part) draws one part's arguments, and reference() takes and returns one part's arrays. A program takes and returns all parts, laid end to end along the dimension named above; an argument that names none is the same for every part. Nothing has to cross between parts.
Inputs may be any that keep to these rules, and one draw needn't show every extreme that they name: partner[i] = i XOR m for one m of 1 .. 3, the same for every i. `tables`: each instance's table names each of its 24 pool blocks exactly once.
All inputs are finite; a program needn't handle non-finite values.
Results may differ from the reference program's by a relative error of at most 0.0061.
Values may be sent and summed in bfloat16 or wider, within the bound.
No kernel may reach another device: no remote copies, remote signals or barrier semaphores. Data moves between devices by JAX's collectives and lax.ppermute only.
A program may use at most 64 MiB of HBM per device.

```python
import jax
import jax.numpy as jnp
from jax import lax

QH = 64
KVH = 8
HD = 128
BLK = 128
REQ = 4
MAXBLK = 6
STEPS = 4
D = 8192
KVD = 1024
LAYERS = 2
CTX = 768
NPOOL = 24
L_MAX = 764
N_INST = 4


def pool_tables(key):
    subkeys = jax.random.split(jax.random.fold_in(key, 11), N_INST)
    perms = jax.vmap(lambda subkey: jax.random.permutation(subkey, NPOOL))(subkeys)
    return perms.reshape(N_INST, REQ, MAXBLK).astype(jnp.int32)


def draw_emb(key, part):
    feats = jnp.arange(D)
    rough = jnp.exp(jax.random.uniform(jax.random.fold_in(key, 21), (D,), jnp.float32, -0.35, 0.35))
    scales = jnp.where(feats < D // 2, 0.6, 1.2) * rough
    noise = jax.random.normal(jax.random.fold_in(key, 22), (STEPS, N_INST * REQ, D), jnp.float32)
    values = noise * scales
    return jnp.clip(values, -24.0, 24.0).astype(jnp.bfloat16)


def draw_out_gain(key, part):
    feats = jnp.arange(D)
    unit = jax.random.uniform(jax.random.fold_in(key, 31), (LAYERS, D), jnp.float32)
    low = jnp.where(feats < D // 2, 0.4, 0.8)
    return (low * jnp.exp(unit * jnp.log(2.0))).astype(jnp.float32)


def draw_k_cache(key, part):
    base = jax.random.normal(jax.random.fold_in(key, 41), (N_INST, LAYERS, NPOOL, BLK, KVD), jnp.float32)
    base = jnp.clip(base, -6.0, 6.0)
    return base.astype(jnp.bfloat16)


def draw_tables(key, part):
    return pool_tables(key)


def draw_lens(key, part):
    values = jax.random.randint(jax.random.fold_in(key, 13), (N_INST * REQ,), 2, L_MAX + 1, jnp.int32)
    longest = jax.random.randint(jax.random.fold_in(key, 14), (), 0, N_INST * REQ, jnp.int32)
    values = values.at[longest].set(L_MAX)
    return values.reshape(N_INST, REQ)


def draw_partner(key, part):
    offset = jax.random.randint(jax.random.fold_in(key, 15), (), 1, N_INST, jnp.int32)
    return jnp.bitwise_xor(jnp.arange(N_INST, dtype=jnp.int32), offset)


def set_ends(array, own_key, low, high):
    spot = [jax.random.randint(jax.random.fold_in(own_key, axis), (), 0, length) for axis, length in enumerate(array.shape)]
    widest = array.shape.index(max(array.shape))
    neighbour = spot[:widest] + [(spot[widest] + 1) % array.shape[widest]] + spot[widest + 1:]
    return array.at[tuple(spot)].set(low).at[tuple(neighbour)].set(high)


def steps_of(key, shape, cuts, smallest, largest):
    level, own = 1.0, jax.random.fold_in(key, 6)
    for position, blocks in cuts:
        heights = jnp.exp(jax.random.uniform(jax.random.fold_in(own, position), (blocks,), jnp.float32, smallest / len(cuts), largest / len(cuts)))
        level = level * jnp.repeat(heights, shape[position] // blocks).reshape([-1 if axis == position else 1 for axis in range(len(shape))])
    return level


def gaussian(own_key, dims, scale, limit, cuts=(), kind=jnp.bfloat16):
    values = jax.random.normal(own_key, dims, jnp.float32) * scale
    if len(cuts) > 0:
        values = steps_of(own_key, dims, cuts, -0.22, 0.18) * values
    return jnp.clip(values, min=-limit, max=limit).astype(kind)


def setup_inputs(seed: int = 0, part: int = 0) -> dict:
    key_list = jax.random.split(jax.random.key(seed), 10)
    own_keys = jax.random.split(jax.random.fold_in(key_list[9], part), 10)
    emb = draw_emb(jax.random.fold_in(jax.random.fold_in(key_list[9], part), 71), part)
    attn_gain = jnp.clip(1.0 + 0.18 * jax.random.normal(key_list[1], (LAYERS, D), jnp.float32), 0.1, 1.9)
    out_gain = draw_out_gain(jax.random.fold_in(key_list[9], 71), part)
    k_cache = draw_k_cache(jax.random.fold_in(jax.random.fold_in(key_list[9], part), 71), part)
    v_cache = gaussian(own_keys[4], (N_INST, LAYERS, NPOOL, BLK, KVD), 1.0, 6.0, ((0, 4), (1, 2), (4, 2)))
    tables = draw_tables(jax.random.fold_in(jax.random.fold_in(key_list[9], part), 71), part)
    lens = draw_lens(jax.random.fold_in(jax.random.fold_in(key_list[9], part), 71), part)
    partner = draw_partner(jax.random.fold_in(key_list[9], 71), part)
    mig_req = set_ends(jax.random.randint(own_keys[8], (N_INST,), 0, REQ), jax.random.fold_in(own_keys[8], 1), 0, REQ - 1).astype(jnp.int32)
    return dict(emb=emb, attn_gain=attn_gain, out_gain=out_gain, k_cache=k_cache, v_cache=v_cache, tables=tables, lens=lens, partner=partner, mig_req=mig_req)


def layer_keys(cache_layer, tables):

    def one_instance(pool_blocks, table_rows):
        return pool_blocks[table_rows.reshape(-1)].reshape(REQ, CTX, KVD)
    return jax.vmap(one_instance)(cache_layer, tables)

def reference(emb, attn_gain, out_gain, k_cache, v_cache, tables, lens, partner, mig_req):
    rows = N_INST * REQ
    group = QH // KVH
    scale = HD ** (-0.5)
    lens_flat = lens.reshape(rows)
    positions = jnp.arange(CTX, dtype=jnp.int32)
    old_mask = positions[None, :] < lens_flat[:, None]
    step_index = jnp.arange(STEPS, dtype=jnp.int32)
    new_keys = jnp.zeros((LAYERS, STEPS, rows, KVD), jnp.bfloat16)
    new_values = jnp.zeros((LAYERS, STEPS, rows, KVD), jnp.bfloat16)
    results = [[None] * STEPS for layer in range(LAYERS)]
    for step in range(STEPS):
        hidden = emb[step]
        for layer in range(LAYERS):
            hidden_f = hidden.astype(jnp.float32)
            squares = lax.optimization_barrier(jnp.sum(hidden_f * hidden_f, axis=-1))
            normed = hidden_f * lax.rsqrt(squares / D + 1e-05)[:, None] * attn_gain[layer]
            heads = normed.reshape(rows, KVH, group, HD)
            query = heads.astype(jnp.bfloat16)
            key_step = lax.optimization_barrier(jnp.mean(heads, axis=2)).reshape(rows, KVD).astype(jnp.bfloat16)
            value_step = lax.optimization_barrier(jnp.mean(hidden_f.reshape(rows, KVH, group, HD), axis=2)).reshape(rows, KVD).astype(jnp.bfloat16)
            new_keys = new_keys.at[layer, step].set(key_step)
            new_values = new_values.at[layer, step].set(value_step)
            keys_old = layer_keys(k_cache[:, layer], tables).reshape(rows, CTX, KVH, HD)
            values_old = layer_keys(v_cache[:, layer], tables).reshape(rows, CTX, KVH, HD)
            keys_fresh = new_keys[layer].reshape(STEPS, rows, KVH, HD)
            values_fresh = new_values[layer].reshape(STEPS, rows, KVH, HD)
            query_f = query.astype(jnp.float32)
            score_old = jnp.einsum('rgqd,rcgd->rgqc', query_f, keys_old.astype(jnp.float32)) * scale
            score_old = jnp.where(old_mask[:, None, None, :], score_old, -jnp.inf)
            score_new = jnp.einsum('rgqd,trgd->rgqt', query_f, keys_fresh.astype(jnp.float32)) * scale
            score_new = jnp.where((step_index <= step)[None, None, None, :], score_new, -jnp.inf)
            top = jnp.maximum(lax.optimization_barrier(jnp.max(score_old, axis=-1)), lax.optimization_barrier(jnp.max(score_new, axis=-1)))
            expo_old = jnp.exp(score_old - top[..., None])
            expo_new = jnp.exp(score_new - top[..., None])
            total = lax.optimization_barrier(jnp.sum(expo_old, axis=-1)) + lax.optimization_barrier(jnp.sum(expo_new, axis=-1))
            weight_old = (expo_old / total[..., None]).astype(jnp.bfloat16)
            weight_new = (expo_new / total[..., None]).astype(jnp.bfloat16)
            attended = jnp.einsum('rgqc,rcgd->rgqd', weight_old.astype(jnp.float32), values_old.astype(jnp.float32))
            attended = attended + jnp.einsum('rgqt,trgd->rgqd', weight_new.astype(jnp.float32), values_fresh.astype(jnp.float32))
            head_norm = attended * lax.rsqrt(lax.optimization_barrier(jnp.mean(attended * attended, axis=-1)) + 1e-05)[..., None]
            hidden = (hidden_f + head_norm.reshape(rows, D) * out_gain[layer]).astype(jnp.bfloat16)
            results[layer][step] = hidden
    layer_out = jnp.stack([jnp.stack(results[layer]) for layer in range(LAYERS)])
    source = partner
    chosen = mig_req[source]
    length = lens[source, chosen]
    flat_index = source * REQ + chosen

    def place(base, piece, start):
        return lax.dynamic_update_slice(base, piece, (start, jnp.int32(0)))
    arrived = []
    for cache, fresh_all in ((k_cache, new_keys), (v_cache, new_values)):
        per_layer = []
        for layer in range(LAYERS):
            logical = layer_keys(cache[:, layer], tables)
            picked = logical[source, chosen]
            picked = jnp.where(positions[None, :, None] < length[:, None, None], picked, jnp.zeros((), picked.dtype))
            fresh = jnp.transpose(fresh_all[layer][:, flat_index], (1, 0, 2))
            per_layer.append(jax.vmap(place)(picked, fresh, length))
        arrived.append(jnp.stack(per_layer, axis=1))
    return (layer_out, arrived[0], arrived[1])
```

```python
import functools

import jax
import jax.numpy as jnp
from jax import lax
from jax.experimental import pallas as pl
from jax.experimental.pallas import tpu as pltpu
from jax.sharding import PartitionSpec as P

QH = 64
KVH = 8
HD = 128
D = 8192
GROUP = QH // KVH
TILE = 16
CHUNK = 64
STEPS = 4
EPS = 1e-05

SMEM = pl.BlockSpec(memory_space=pltpu.SMEM)
VMEM = pl.BlockSpec(memory_space=pltpu.VMEM)
ANY = pl.BlockSpec(memory_space=pl.ANY)


def params(mib):
    return pltpu.CompilerParams(vmem_limit_bytes=mib << 20)


def row_counts(offset, instances, sections, context):
    crossing = max(
        sum(1 for i in range(instances) if i <= cut < i ^ offset) for cut in range(instances)
    )
    if instances * sections > 8:
        shares = (12,)
    elif crossing == 1:
        shares = (9, 12)
    else:
        shares = (4, 6, 8, 9, 10, 11, 12)
    return sorted({-(-context * share // (12 * CHUNK)) * CHUNK for share in shares})


def pick_kernel(counts, lens_ref, mig_ref, partner_ref, choice_ref):
    instance = lax.axis_index("inst")
    other = partner_ref[instance]
    offset = partner_ref[0]
    longest = jnp.maximum(
        lens_ref[instance, mig_ref[instance]], lens_ref[other, mig_ref[other]]
    )
    choice = jnp.int32(0)
    for known, edges in counts:
        for i, edge in enumerate(edges):
            behind = offset > known
            if i + 1 < len(edges):
                behind = jnp.logical_or(
                    behind, jnp.logical_and(offset == known, longest > edge)
                )
            choice = choice + jnp.where(behind, 1, 0)
    choice_ref[0] = choice


def gather_kernel(rows, tables_ref, mig_ref, k_ref, v_ref, out_ref, sems):
    request = mig_ref[lax.axis_index("inst")]
    block_tok, width = k_ref.shape[3:]
    copies = []
    for j in range(-(-rows // block_tok)):
        block = tables_ref[0, request, j]
        count = min(block_tok, rows - j * block_tok)
        for side, cache in enumerate((k_ref, v_ref)):
            copies.append(
                pltpu.make_async_copy(
                    cache.at[0, 0, block, pl.ds(0, count), :],
                    out_ref.at[pl.ds(j * block_tok, count), pl.ds(side * width, width)],
                    sems.at[side, j],
                )
            )
    for copy in copies:
        copy.start()
    for copy in copies:
        copy.wait()


def layer_kernel(
    phase, first, peers, tables_ref, lens_ref, mig_ref, hid_ref, gain_ref, out_gain_ref,
    k_ref, v_ref, *rest
):
    other_refs, rest = rest[:peers], rest[peers:]
    if not first:
        rest = rest[2:]
    out_ref, fresh_ref, hid, x, kn, vn, o, out, fresh, o_sem = rest
    steps, requests, width = hid_ref.shape
    block_tok, kv_width = k_ref.shape[3:]
    blocks = tables_ref.shape[2]
    groups = kv_width // HD
    rows = GROUP * steps
    scale = HD ** (-0.5)

    @pl.when(lax.axis_index("section") == phase)
    def _():
        instance = lax.axis_index("inst")
        handed = mig_ref[instance]
        for t in range(steps):
            mine = hid_ref[t].astype(jnp.float32)
            total = jnp.sum(mine * mine, axis=-1, keepdims=True)
            for other_ref in other_refs:
                theirs = other_ref[t].astype(jnp.float32)
                total = total + jnp.sum(theirs * theirs, axis=-1, keepdims=True)
            normed = mine * lax.rsqrt(total / D + EPS) * gain_ref[...]
            span = pl.ds(t * requests, requests)
            for head in range(groups * GROUP):
                hid[head, span, :] = mine[:, head * HD : (head + 1) * HD]
                x[head, span, :] = normed[:, head * HD : (head + 1) * HD]
        for g in range(groups):
            for source, target in ((x, kn), (hid, vn)):
                summed = source[g * GROUP]
                for h in range(1, GROUP):
                    summed = summed + source[g * GROUP + h]
                target[g] = summed * (1.0 / GROUP)

        lines = groups * rows
        position = lax.broadcasted_iota(jnp.int32, (lines, blocks * block_tok), 1)
        new_step = lax.broadcasted_iota(jnp.int32, (lines, TILE), 1)
        own_step = lax.rem(lax.broadcasted_iota(jnp.int32, (lines, TILE), 0), steps)
        new_mask = new_step <= own_step
        none = jnp.zeros((rows, HD), jnp.float32)
        blank = jnp.zeros((TILE - steps, kv_width), jnp.float32)

        def newest(source, request):
            every = [source[g, pl.ds(request, steps, stride=requests), :] for g in range(groups)]
            return jnp.concatenate([jnp.concatenate(every, axis=1), blank], axis=0).astype(
                jnp.bfloat16
            )

        fresh[:, pl.ds(0, kv_width)] = newest(kn, handed)
        fresh[:, pl.ds(kv_width, kv_width)] = newest(vn, handed)

        for r in range(requests):
            here = pl.ds(r, steps, stride=requests)
            mask = position < lens_ref[instance, r]
            at = [tables_ref[0, r, j] for j in range(blocks)]
            new_k, new_v = newest(kn, r), newest(vn, r)
            old_k, old_v = [
                jnp.concatenate([cache[0, 0, at[j]] for j in range(blocks)], axis=0)
                for cache in (k_ref, v_ref)
            ]
            stripes = []
            for g in range(groups):
                query = [x[g * GROUP + h, here, :] for h in range(GROUP)]
                stripe = [none] * groups
                stripe[g] = jnp.concatenate(query, axis=0)
                stripes.append(jnp.concatenate(stripe, axis=1))
            query = jnp.concatenate(stripes, axis=0).astype(jnp.bfloat16)
            score, score_new = [
                scale
                * lax.dot_general(
                    query, key, (((1,), (1,)), ((), ())), preferred_element_type=jnp.float32
                )
                for key in (old_k, new_k)
            ]
            score = jnp.where(mask, score, -jnp.inf)
            score_new = jnp.where(new_mask, score_new, -jnp.inf)
            top = jnp.maximum(
                jnp.max(score, axis=-1, keepdims=True), jnp.max(score_new, axis=-1, keepdims=True)
            )
            expo = jnp.exp(score - top)
            expo_new = jnp.exp(score_new - top)
            total = jnp.sum(expo, axis=-1, keepdims=True) + jnp.sum(
                expo_new, axis=-1, keepdims=True
            )
            weight = (expo / total).astype(jnp.bfloat16)
            weight_new = (expo_new / total).astype(jnp.bfloat16)
            every = jnp.dot(weight, old_v, preferred_element_type=jnp.float32) + jnp.dot(
                weight_new, new_v, preferred_element_type=jnp.float32
            )
            for g in range(groups):
                attended = every[g * rows : (g + 1) * rows, g * HD : (g + 1) * HD]
                attended = attended * lax.rsqrt(
                    jnp.mean(attended * attended, axis=-1, keepdims=True) + EPS
                )
                for h in range(GROUP):
                    o[g * GROUP + h, here, :] = attended[h * steps : (h + 1) * steps]

        for t in range(steps):
            span = pl.ds(t * requests, requests)
            for head in range(groups * GROUP):
                lanes = pl.ds(head * HD, HD)
                out[0, t, :, lanes] = (
                    hid[head, span, :] + o[head, span, :] * out_gain_ref[:, lanes]
                ).astype(jnp.bfloat16)
        sends = [
            pltpu.make_async_copy(out, out_ref, o_sem.at[0]),
            pltpu.make_async_copy(fresh, fresh_ref, o_sem.at[1]),
        ]
        for copy in sends:
            copy.start()
        for copy in sends:
            copy.wait()


@functools.partial(jax.jit, static_argnums=0)
def layer(
    phase, tables, lens, mig_req, hidden, others, attn_gain, out_gain, k_cache, v_cache, prior
):
    steps, requests, width = hidden.shape
    block_tok, kv_width = k_cache.shape[3:]
    context = tables.shape[2] * block_tok
    lines = steps * requests
    heads = width // HD
    groups = kv_width // HD
    out_shape = (
        jax.ShapeDtypeStruct((1, steps, requests, width), jnp.bfloat16),
        jax.ShapeDtypeStruct((TILE, 2 * kv_width), jnp.bfloat16),
    )
    operands = (tables, lens, mig_req, hidden, attn_gain, out_gain, k_cache, v_cache)
    operands += others + prior
    placed = len(operands) - len(prior)
    return pl.pallas_call(
        functools.partial(layer_kernel, phase, not prior, len(others)),
        out_shape=out_shape,
        in_specs=[SMEM] * 3 + [VMEM] * (5 + len(others)) + [ANY] * len(prior),
        out_specs=(ANY, ANY),
        input_output_aliases={placed + i: i for i in range(len(prior))},
        scratch_shapes=[
            pltpu.VMEM((heads, lines, HD), jnp.float32),
            pltpu.VMEM((heads, lines, HD), jnp.float32),
            pltpu.VMEM((groups, lines, HD), jnp.float32),
            pltpu.VMEM((groups, lines, HD), jnp.float32),
            pltpu.VMEM((heads, lines, HD), jnp.float32),
            pltpu.VMEM((1, steps, requests, width), jnp.bfloat16),
            pltpu.VMEM((TILE, 2 * kv_width), jnp.bfloat16),
            pltpu.SemaphoreType.DMA((2,)),
        ],
        compiler_params=params(32),
        cost_estimate=pl.CostEstimate(
            flops=4 * lines * width * context, bytes_accessed=4 * requests * context * kv_width,
            transcendentals=lines * width * context // HD,
        ),
        name=f"layer_{phase}",
    )(*operands)


def place_kernel(
    rows, lens_ref, mig_ref, partner_ref, got_ref, fresh_ref, k_ref, v_ref,
    edge, blank, sems, fetch_sems, store_sems
):
    source = partner_ref[lax.axis_index("inst")]
    length = lens_ref[source, mig_ref[source]]
    context, width = k_ref.shape[2:]
    chunks = context // CHUNK
    border = length // CHUNK
    sides = tuple(enumerate((k_ref, v_ref)))

    fetches = [
        pltpu.make_async_copy(
            got_ref.at[
                pl.ds(jnp.minimum(border, rows // CHUNK - 1) * CHUNK, CHUNK),
                pl.ds(side * width, width),
            ],
            edge.at[side, pl.ds(0, CHUNK), :],
            fetch_sems.at[side],
        )
        for side, _ in sides
    ]
    for fetch in fetches:
        fetch.start()
    blank[...] = jnp.zeros_like(blank)

    def put(side, target, c):
        span = pl.ds(c * CHUNK, CHUNK)
        here = target.at[0, 0, span, :]
        clear = pltpu.make_async_copy(blank, here, sems.at[side, c])
        if (c + 1) * CHUNK > rows:
            return None, clear
        lanes = pl.ds(side * width, width)
        return pltpu.make_async_copy(got_ref.at[span, lanes], here, sems.at[side, c]), clear

    def each(wait):
        for c in range(chunks):
            for side, target in sides:
                move, clear = put(side, target, c)
                if move is not None:
                    pl.when(c < border)(move.wait if wait else move.start)
                pl.when(c > border + 1)(clear.wait if wait else clear.start)

    each(False)
    stores = []
    for side, target in sides:
        fetches[side].wait()
        place = border * CHUNK + lax.broadcasted_iota(jnp.int32, (2 * CHUNK, width), 0)
        block = jnp.concatenate(
            [edge[side, :CHUNK].astype(jnp.float32), jnp.zeros((CHUNK, width), jnp.float32)], axis=0
        )
        block = jnp.where(place < length, block, 0.0)
        new = fresh_ref[:, pl.ds(side * width, width)].astype(jnp.float32)
        for t in range(STEPS):
            block = jnp.where(place == length + t, new[t : t + 1], block)
        edge[side] = block.astype(jnp.bfloat16)
        for half in range(2):
            stores.append(
                pltpu.make_async_copy(
                    edge.at[side, pl.ds(half * CHUNK, CHUNK), :],
                    target.at[
                        0, 0, pl.ds(jnp.minimum(border + half, chunks - 1) * CHUNK, CHUNK), :
                    ],
                    store_sems.at[side, half],
                )
            )
            if half == 0:
                stores[-1].start()
            else:
                pl.when(border + 1 < chunks)(stores[-1].start)
    for i, store in enumerate(stores):
        if i % 2 == 0:
            store.wait()
        else:
            pl.when(border + 1 < chunks)(store.wait)
    each(True)


@functools.partial(jax.jit, static_argnums=0)
def place(context, lens, mig_req, partner, got, fresh):
    rows = got.shape[0]
    width = got.shape[1] // 2
    shape = jax.ShapeDtypeStruct((1, 1, context, width), jnp.bfloat16)
    return pl.pallas_call(
        functools.partial(place_kernel, rows),
        out_shape=(shape, shape),
        in_specs=[SMEM] * 3 + [ANY, VMEM],
        out_specs=(ANY, ANY),
        scratch_shapes=[
            pltpu.VMEM((2, 2 * CHUNK, width), jnp.bfloat16),
            pltpu.VMEM((CHUNK, width), jnp.bfloat16),
            pltpu.SemaphoreType.DMA((2, context // CHUNK)),
            pltpu.SemaphoreType.DMA((2,)),
            pltpu.SemaphoreType.DMA((2, 2)),
        ],
        compiler_params=params(8),
        name="place",
    )(lens, mig_req, partner, got, fresh)


@functools.partial(jax.jit, static_argnums=0)
def gather(rows, tables, mig_req, k_cache, v_cache):
    block_tok, kv_width = k_cache.shape[3:]
    return pl.pallas_call(
        functools.partial(gather_kernel, rows),
        out_shape=jax.ShapeDtypeStruct((rows, 2 * kv_width), jnp.bfloat16),
        in_specs=[SMEM, SMEM, ANY, ANY],
        out_specs=ANY,
        scratch_shapes=[pltpu.SemaphoreType.DMA((2, -(-rows // block_tok)))],
        compiler_params=params(8),
        name="gather",
    )(tables, mig_req, k_cache, v_cache)


def branch(offset, rows, context):
    def run(emb, attn_gain, out_gain, k_cache, v_cache, tables, lens, partner, mig_req):
        sections = lax.axis_size("section")
        tp = lax.axis_size("tp")
        pairs = [(i, i ^ offset) for i in range(lax.axis_size("inst"))]
        handed = gather(rows, tables, mig_req, k_cache, v_cache)
        got = lax.ppermute(handed, "inst", pairs)
        hidden, prior = emb, ()
        for phase in range(sections):
            if phase > 0:
                hidden = lax.ppermute(prior[0], "section", [(phase - 1, phase)])[0]
            others = tuple(
                lax.ppermute(hidden, "tp", [(i, (i + by) % tp) for i in range(tp)])
                for by in range(1, tp)
            )
            prior = tuple(
                layer(
                    phase, tables, lens, mig_req, hidden, others, attn_gain, out_gain,
                    k_cache, v_cache, prior,
                )
            )
        fresh = lax.ppermute(prior[1], "inst", pairs)
        arrived = place(context, lens, mig_req, partner, got, fresh)
        return (prior[0], arrived[0], arrived[1])

    return run


def local(emb, attn_gain, out_gain, k_cache, v_cache, tables, lens, partner, mig_req):
    instances, sections = lax.axis_size("inst"), lax.axis_size("section")
    context = tables.shape[2] * k_cache.shape[3]
    counts = tuple(
        (offset, row_counts(offset, instances, sections, context))
        for offset in range(1, instances)
    )
    choice = pl.pallas_call(
        functools.partial(pick_kernel, counts),
        out_shape=jax.ShapeDtypeStruct((1,), jnp.int32),
        in_specs=[SMEM] * 3,
        out_specs=SMEM,
        name="pick",
    )(lens, mig_req, partner)
    branches = [branch(offset, rows, context) for offset, edges in counts for rows in edges]
    return lax.switch(
        choice[0], branches, emb, attn_gain, out_gain, k_cache, v_cache, tables, lens, partner,
        mig_req,
    )


def solution(mesh):
    return jax.shard_map(
        local,
        mesh=mesh,
        in_specs=(
            P(None, ("groups", "inst"), "tp"),
            P("section", "tp"),
            P("section", "tp"),
            P(("groups", "inst"), "section", None, None, "tp"),
            P(("groups", "inst"), "section", None, None, "tp"),
            P(("groups", "inst"), None, None),
            P("groups", None),
            P(),
            P("groups"),
        ),
        out_specs=(
            P("section", None, ("groups", "inst"), "tp"),
            P(("groups", "inst"), "section", None, "tp"),
            P(("groups", "inst"), "section", None, "tp"),
        ),
        check_vma=False,
    )
```

```python
import functools

import jax
import jax.numpy as jnp
from jax import lax
from jax.experimental import pallas as pl
from jax.experimental.pallas import tpu as pltpu
from jax.sharding import PartitionSpec as P

QH = 64
KVH = 8
HD = 128
D = 8192
GROUP = QH // KVH
TILE = 16
CHUNK = 64
STEPS = 4
EPS = 1e-05

SMEM = pl.BlockSpec(memory_space=pltpu.SMEM)
VMEM = pl.BlockSpec(memory_space=pltpu.VMEM)
ANY = pl.BlockSpec(memory_space=pl.ANY)


def params(mib):
    return pltpu.CompilerParams(vmem_limit_bytes=mib << 20)


def row_counts(offset, instances, sections, context):
    crossing = max(
        sum(1 for i in range(instances) if i <= cut < i ^ offset) for cut in range(instances)
    )
    if instances * sections > 8:
        shares = (12,)
    elif crossing == 1:
        shares = (12,)
    else:
        shares = (4, 6, 8, 9, 10, 11, 12)
    return sorted({-(-context * share // (12 * CHUNK)) * CHUNK for share in shares})


def pick_kernel(counts, lens_ref, mig_ref, partner_ref, choice_ref):
    instance = lax.axis_index("inst")
    other = partner_ref[instance]
    offset = partner_ref[0]
    longest = jnp.maximum(
        lens_ref[instance, mig_ref[instance]], lens_ref[other, mig_ref[other]]
    )
    choice = jnp.int32(0)
    for known, edges in counts:
        for i, edge in enumerate(edges):
            behind = offset > known
            if i + 1 < len(edges):
                behind = jnp.logical_or(
                    behind, jnp.logical_and(offset == known, longest > edge)
                )
            choice = choice + jnp.where(behind, 1, 0)
    choice_ref[0] = choice


def gather_kernel(rows, tables_ref, mig_ref, k_ref, v_ref, out_ref, sems):
    request = mig_ref[lax.axis_index("inst")]
    block_tok, width = k_ref.shape[3:]
    parts = block_tok // CHUNK

    def copies(c):
        block = tables_ref[0, request, lax.div(c, parts)]
        span = pl.ds(pl.multiple_of(lax.rem(c, parts) * CHUNK, CHUNK), CHUNK)
        place = pl.ds(pl.multiple_of(c * CHUNK, CHUNK), CHUNK)
        return [
            pltpu.make_async_copy(
                cache.at[0, 0, block, span, :],
                out_ref.at[place, pl.ds(side * width, width)],
                sems.at[side, c],
            )
            for side, cache in enumerate((k_ref, v_ref))
        ]

    @pl.loop(0, rows // CHUNK)
    def _(c):
        for copy in copies(c):
            copy.start()

    @pl.loop(0, rows // CHUNK)
    def _(c):
        for copy in copies(c):
            copy.wait()


def layer_kernel(
    peers, phase_ref, tables_ref, lens_ref, mig_ref, hid_ref, gain_ref, out_gain_ref,
    k_ref, v_ref, *rest
):
    other_refs, rest = rest[:peers], rest[peers + 2 :]
    out_ref, fresh_ref, hid, x, kn, vn, o, out, fresh, o_sem = rest
    steps, requests, width = hid_ref.shape
    block_tok, kv_width = k_ref.shape[3:]
    blocks = tables_ref.shape[2]
    groups = kv_width // HD
    rows = GROUP * steps
    scale = HD ** (-0.5)

    @pl.when(lax.axis_index("section") == phase_ref[0])
    def _():
        instance = lax.axis_index("inst")
        handed = mig_ref[instance]
        for t in range(steps):
            mine = hid_ref[t].astype(jnp.float32)
            total = jnp.sum(mine * mine, axis=-1, keepdims=True)
            for other_ref in other_refs:
                theirs = other_ref[t].astype(jnp.float32)
                total = total + jnp.sum(theirs * theirs, axis=-1, keepdims=True)
            normed = mine * lax.rsqrt(total / D + EPS) * gain_ref[...]
            span = pl.ds(t * requests, requests)
            for head in range(groups * GROUP):
                hid[head, span, :] = mine[:, head * HD : (head + 1) * HD]
                x[head, span, :] = normed[:, head * HD : (head + 1) * HD]
        for g in range(groups):
            for source, target in ((x, kn), (hid, vn)):
                summed = source[g * GROUP]
                for h in range(1, GROUP):
                    summed = summed + source[g * GROUP + h]
                target[g] = summed * (1.0 / GROUP)

        lines = groups * rows
        position = lax.broadcasted_iota(jnp.int32, (lines, blocks * block_tok), 1)
        new_step = lax.broadcasted_iota(jnp.int32, (lines, TILE), 1)
        own_step = lax.rem(lax.broadcasted_iota(jnp.int32, (lines, TILE), 0), steps)
        new_mask = new_step <= own_step
        none = jnp.zeros((rows, HD), jnp.float32)
        blank = jnp.zeros((TILE - steps, kv_width), jnp.float32)

        def newest(source, request):
            every = [source[g, pl.ds(request, steps, stride=requests), :] for g in range(groups)]
            return jnp.concatenate([jnp.concatenate(every, axis=1), blank], axis=0).astype(
                jnp.bfloat16
            )

        fresh[:, pl.ds(0, kv_width)] = newest(kn, handed)
        fresh[:, pl.ds(kv_width, kv_width)] = newest(vn, handed)

        @pl.loop(0, requests)
        def _(r):
            here = pl.ds(r, steps, stride=requests)
            mask = position < lens_ref[instance, r]
            at = [tables_ref[0, r, j] for j in range(blocks)]
            new_k, new_v = newest(kn, r), newest(vn, r)
            old_k, old_v = [
                jnp.concatenate([cache[0, 0, at[j]] for j in range(blocks)], axis=0)
                for cache in (k_ref, v_ref)
            ]
            stripes = []
            for g in range(groups):
                query = [x[g * GROUP + h, here, :] for h in range(GROUP)]
                stripe = [none] * groups
                stripe[g] = jnp.concatenate(query, axis=0)
                stripes.append(jnp.concatenate(stripe, axis=1))
            query = jnp.concatenate(stripes, axis=0).astype(jnp.bfloat16)
            score, score_new = [
                scale
                * lax.dot_general(
                    query, key, (((1,), (1,)), ((), ())), preferred_element_type=jnp.float32
                )
                for key in (old_k, new_k)
            ]
            score = jnp.where(mask, score, -jnp.inf)
            score_new = jnp.where(new_mask, score_new, -jnp.inf)
            top = jnp.maximum(
                jnp.max(score, axis=-1, keepdims=True), jnp.max(score_new, axis=-1, keepdims=True)
            )
            expo = jnp.exp(score - top)
            expo_new = jnp.exp(score_new - top)
            total = jnp.sum(expo, axis=-1, keepdims=True) + jnp.sum(
                expo_new, axis=-1, keepdims=True
            )
            weight = (expo / total).astype(jnp.bfloat16)
            weight_new = (expo_new / total).astype(jnp.bfloat16)
            every = jnp.dot(weight, old_v, preferred_element_type=jnp.float32) + jnp.dot(
                weight_new, new_v, preferred_element_type=jnp.float32
            )
            for g in range(groups):
                attended = every[g * rows : (g + 1) * rows, g * HD : (g + 1) * HD]
                attended = attended * lax.rsqrt(
                    jnp.mean(attended * attended, axis=-1, keepdims=True) + EPS
                )
                for h in range(GROUP):
                    o[g * GROUP + h, here, :] = attended[h * steps : (h + 1) * steps]

        for t in range(steps):
            span = pl.ds(t * requests, requests)
            for head in range(groups * GROUP):
                lanes = pl.ds(head * HD, HD)
                out[0, t, :, lanes] = (
                    hid[head, span, :] + o[head, span, :] * out_gain_ref[:, lanes]
                ).astype(jnp.bfloat16)
        sends = [
            pltpu.make_async_copy(out, out_ref, o_sem.at[0]),
            pltpu.make_async_copy(fresh, fresh_ref, o_sem.at[1]),
        ]
        for copy in sends:
            copy.start()
        for copy in sends:
            copy.wait()


@jax.jit
def layer(
    phase, tables, lens, mig_req, hidden, others, attn_gain, out_gain, k_cache, v_cache, prior
):
    steps, requests, width = hidden.shape
    block_tok, kv_width = k_cache.shape[3:]
    context = tables.shape[2] * block_tok
    lines = steps * requests
    heads = width // HD
    groups = kv_width // HD
    out_shape = (
        jax.ShapeDtypeStruct((1, steps, requests, width), jnp.bfloat16),
        jax.ShapeDtypeStruct((TILE, 2 * kv_width), jnp.bfloat16),
    )
    operands = (
        phase.reshape(1), tables, lens, mig_req, hidden, attn_gain, out_gain, k_cache, v_cache
    )
    operands += others + prior
    placed = len(operands) - len(prior)
    return pl.pallas_call(
        functools.partial(layer_kernel, len(others)),
        out_shape=out_shape,
        in_specs=[SMEM] * 4 + [VMEM] * (5 + len(others)) + [ANY] * len(prior),
        out_specs=(ANY, ANY),
        input_output_aliases={placed + i: i for i in range(len(prior))},
        scratch_shapes=[
            pltpu.VMEM((heads, lines, HD), jnp.float32),
            pltpu.VMEM((heads, lines, HD), jnp.float32),
            pltpu.VMEM((groups, lines, HD), jnp.float32),
            pltpu.VMEM((groups, lines, HD), jnp.float32),
            pltpu.VMEM((heads, lines, HD), jnp.float32),
            pltpu.VMEM((1, steps, requests, width), jnp.bfloat16),
            pltpu.VMEM((TILE, 2 * kv_width), jnp.bfloat16),
            pltpu.SemaphoreType.DMA((2,)),
        ],
        compiler_params=params(32),
        cost_estimate=pl.CostEstimate(
            flops=4 * lines * width * context, bytes_accessed=4 * requests * context * kv_width,
            transcendentals=lines * width * context // HD,
        ),
        name="layer",
    )(*operands)


def place_kernel(
    rows, lens_ref, mig_ref, partner_ref, got_ref, fresh_ref, k_ref, v_ref,
    edge, blank, sems, fetch_sems, store_sems
):
    source = partner_ref[lax.axis_index("inst")]
    length = lens_ref[source, mig_ref[source]]
    context, width = k_ref.shape[2:]
    chunks = context // CHUNK
    border = length // CHUNK
    sides = tuple(enumerate((k_ref, v_ref)))

    fetches = [
        pltpu.make_async_copy(
            got_ref.at[
                pl.ds(pl.multiple_of(jnp.minimum(border, rows // CHUNK - 1) * CHUNK, CHUNK), CHUNK),
                pl.ds(side * width, width),
            ],
            edge.at[side, pl.ds(0, CHUNK), :],
            fetch_sems.at[side],
        )
        for side, _ in sides
    ]
    for fetch in fetches:
        fetch.start()
    blank[...] = jnp.zeros_like(blank)

    def moves(c):
        span = pl.ds(pl.multiple_of(c * CHUNK, CHUNK), CHUNK)
        return [
            pltpu.make_async_copy(
                got_ref.at[span, pl.ds(side * width, width)],
                target.at[0, 0, span, :],
                sems.at[side, c],
            )
            for side, target in sides
        ]

    def clears(c):
        span = pl.ds(pl.multiple_of(c * CHUNK, CHUNK), CHUNK)
        return [
            pltpu.make_async_copy(blank, target.at[0, 0, span, :], sems.at[side, c])
            for side, target in sides
        ]

    @pl.loop(0, border)
    def _(c):
        for copy in moves(c):
            copy.start()

    @pl.loop(border + 2, chunks)
    def _(c):
        for copy in clears(c):
            copy.start()

    stores = []
    for side, target in sides:
        fetches[side].wait()
        place = border * CHUNK + lax.broadcasted_iota(jnp.int32, (2 * CHUNK, width), 0)
        block = jnp.concatenate(
            [edge[side, :CHUNK].astype(jnp.float32), jnp.zeros((CHUNK, width), jnp.float32)], axis=0
        )
        block = jnp.where(place < length, block, 0.0)
        new = fresh_ref[:, pl.ds(side * width, width)].astype(jnp.float32)
        for t in range(STEPS):
            block = jnp.where(place == length + t, new[t : t + 1], block)
        edge[side] = block.astype(jnp.bfloat16)
        for half in range(2):
            stores.append(
                pltpu.make_async_copy(
                    edge.at[side, pl.ds(half * CHUNK, CHUNK), :],
                    target.at[
                        0, 0, pl.ds(jnp.minimum(border + half, chunks - 1) * CHUNK, CHUNK), :
                    ],
                    store_sems.at[side, half],
                )
            )
            if half == 0:
                stores[-1].start()
            else:
                pl.when(border + 1 < chunks)(stores[-1].start)
    for i, store in enumerate(stores):
        if i % 2 == 0:
            store.wait()
        else:
            pl.when(border + 1 < chunks)(store.wait)

    @pl.loop(0, border)
    def _(c):
        for copy in moves(c):
            copy.wait()

    @pl.loop(border + 2, chunks)
    def _(c):
        for copy in clears(c):
            copy.wait()


@functools.partial(jax.jit, static_argnums=0)
def place(context, lens, mig_req, partner, got, fresh):
    rows = got.shape[0]
    width = got.shape[1] // 2
    shape = jax.ShapeDtypeStruct((1, 1, context, width), jnp.bfloat16)
    return pl.pallas_call(
        functools.partial(place_kernel, rows),
        out_shape=(shape, shape),
        in_specs=[SMEM] * 3 + [ANY, VMEM],
        out_specs=(ANY, ANY),
        scratch_shapes=[
            pltpu.VMEM((2, 2 * CHUNK, width), jnp.bfloat16),
            pltpu.VMEM((CHUNK, width), jnp.bfloat16),
            pltpu.SemaphoreType.DMA((2, context // CHUNK)),
            pltpu.SemaphoreType.DMA((2,)),
            pltpu.SemaphoreType.DMA((2, 2)),
        ],
        compiler_params=params(8),
        name="place",
    )(lens, mig_req, partner, got, fresh)


@functools.partial(jax.jit, static_argnums=0)
def gather(rows, tables, mig_req, k_cache, v_cache):
    kv_width = k_cache.shape[4]
    return pl.pallas_call(
        functools.partial(gather_kernel, rows),
        out_shape=jax.ShapeDtypeStruct((rows, 2 * kv_width), jnp.bfloat16),
        in_specs=[SMEM, SMEM, ANY, ANY],
        out_specs=ANY,
        scratch_shapes=[pltpu.SemaphoreType.DMA((2, rows // CHUNK))],
        compiler_params=params(8),
        name="gather",
    )(tables, mig_req, k_cache, v_cache)


def branch(offset, rows, context):
    def run(emb, attn_gain, out_gain, k_cache, v_cache, tables, lens, partner, mig_req):
        sections = lax.axis_size("section")
        tp = lax.axis_size("tp")
        pairs = [(i, i ^ offset) for i in range(lax.axis_size("inst"))]
        handed = gather(rows, tables, mig_req, k_cache, v_cache)
        got = lax.ppermute(handed, "inst", pairs)

        def phase(number, carry):
            hidden, prior = carry
            others = tuple(
                lax.ppermute(hidden, "tp", [(i, (i + by) % tp) for i in range(tp)])
                for by in range(1, tp)
            )
            prior = tuple(
                layer(
                    number, tables, lens, mig_req, hidden, others, attn_gain, out_gain,
                    k_cache, v_cache, prior,
                )
            )
            onward = [(i, i + 1) for i in range(sections - 1)]
            return lax.ppermute(prior[0], "section", onward)[0], prior

        empty = (
            jnp.zeros((1,) + emb.shape, emb.dtype),
            jnp.zeros((TILE, 2 * k_cache.shape[4]), k_cache.dtype),
        )
        _, prior = lax.fori_loop(0, sections, phase, (emb, empty))
        fresh = lax.ppermute(prior[1], "inst", pairs)
        arrived = place(context, lens, mig_req, partner, got, fresh)
        return (prior[0], arrived[0], arrived[1])

    return run


def local(emb, attn_gain, out_gain, k_cache, v_cache, tables, lens, partner, mig_req):
    instances, sections = lax.axis_size("inst"), lax.axis_size("section")
    context = tables.shape[2] * k_cache.shape[3]
    counts = tuple(
        (offset, row_counts(offset, instances, sections, context))
        for offset in range(1, instances)
    )
    choice = pl.pallas_call(
        functools.partial(pick_kernel, counts),
        out_shape=jax.ShapeDtypeStruct((1,), jnp.int32),
        in_specs=[SMEM] * 3,
        out_specs=SMEM,
        name="pick",
    )(lens, mig_req, partner)
    branches = [branch(offset, rows, context) for offset, edges in counts for rows in edges]
    return lax.switch(
        choice[0], branches, emb, attn_gain, out_gain, k_cache, v_cache, tables, lens, partner,
        mig_req,
    )


def solution(mesh):
    return jax.shard_map(
        local,
        mesh=mesh,
        in_specs=(
            P(None, ("groups", "inst"), "tp"),
            P("section", "tp"),
            P("section", "tp"),
            P(("groups", "inst"), "section", None, None, "tp"),
            P(("groups", "inst"), "section", None, None, "tp"),
            P(("groups", "inst"), None, None),
            P("groups", None),
            P(),
            P("groups"),
        ),
        out_specs=(
            P("section", None, ("groups", "inst"), "tp"),
            P(("groups", "inst"), "section", None, "tp"),
            P(("groups", "inst"), "section", None, "tp"),
        ),
        check_vma=False,
    )
```

```python
import functools

import jax
import jax.numpy as jnp
from jax import lax
from jax.experimental import pallas as pl
from jax.experimental.pallas import tpu as pltpu
from jax.sharding import PartitionSpec as P

QH = 64
KVH = 8
HD = 128
D = 8192
GROUP = QH // KVH
TILE = 16
CHUNK = 64
STEPS = 4
FINE = 32
EPS = 1e-05

SMEM = pl.BlockSpec(memory_space=pltpu.SMEM)
VMEM = pl.BlockSpec(memory_space=pltpu.VMEM)
ANY = pl.BlockSpec(memory_space=pl.ANY)


def params(mib):
    return pltpu.CompilerParams(vmem_limit_bytes=mib << 20)


def row_counts(offset, instances, sections, context):
    crossing = max(
        sum(1 for i in range(instances) if i <= cut < i ^ offset) for cut in range(instances)
    )
    lowest = context
    if crossing == 2 and instances * sections <= 8:
        lowest = -(-context * 5 // (12 * CHUNK)) * CHUNK
    return list(range(lowest, context, FINE)) + [context]


def pick_kernel(counts, lens_ref, mig_ref, partner_ref, choice_ref):
    instance = lax.axis_index("inst")
    other = partner_ref[instance]
    longest = jnp.maximum(
        lens_ref[instance, mig_ref[instance]], lens_ref[other, mig_ref[other]]
    )
    choice = jnp.int32(0)
    for count in counts[:-1]:
        choice = choice + jnp.where(longest > count, 1, 0)
    choice_ref[0] = choice


@functools.partial(jax.jit, static_argnums=0)
def pick(counts, lens, mig_req, partner):
    return pl.pallas_call(
        functools.partial(pick_kernel, counts),
        out_shape=jax.ShapeDtypeStruct((1,), jnp.int32),
        in_specs=[SMEM] * 3,
        out_specs=SMEM,
        name="pick",
    )(lens, mig_req, partner)[0]


def gather_kernel(start, rows, tables_ref, mig_ref, k_ref, v_ref, out_ref, sems):
    request = mig_ref[lax.axis_index("inst")]
    block_tok, width = k_ref.shape[3:]
    parts = block_tok // CHUNK

    def copies(c):
        at = c + start // CHUNK
        block = tables_ref[0, request, lax.div(at, parts)]
        span = pl.ds(pl.multiple_of(lax.rem(at, parts) * CHUNK, CHUNK), CHUNK)
        place = pl.ds(pl.multiple_of(c * CHUNK, CHUNK), CHUNK)
        return [
            pltpu.make_async_copy(
                cache.at[0, 0, block, span, :],
                out_ref.at[place, pl.ds(side * width, width)],
                sems.at[side, c],
            )
            for side, cache in enumerate((k_ref, v_ref))
        ]

    @pl.loop(0, rows // CHUNK)
    def _(c):
        for copy in copies(c):
            copy.start()

    @pl.loop(0, rows // CHUNK)
    def _(c):
        for copy in copies(c):
            copy.wait()


def layer_kernel(
    phase, first, peers, tables_ref, lens_ref, mig_ref, hid_ref, gain_ref, out_gain_ref,
    k_ref, v_ref, *rest
):
    other_refs, rest = rest[:peers], rest[peers:]
    if not first:
        rest = rest[2:]
    out_ref, fresh_ref, hid, x, kn, vn, o, out, fresh, o_sem = rest
    steps, requests, width = hid_ref.shape
    block_tok, kv_width = k_ref.shape[3:]
    blocks = tables_ref.shape[2]
    groups = kv_width // HD
    rows = GROUP * steps
    scale = HD ** (-0.5)

    @pl.when(lax.axis_index("section") == phase)
    def _():
        instance = lax.axis_index("inst")
        handed = mig_ref[instance]
        for t in range(steps):
            mine = hid_ref[t].astype(jnp.float32)
            total = jnp.sum(mine * mine, axis=-1, keepdims=True)
            for other_ref in other_refs:
                theirs = other_ref[t].astype(jnp.float32)
                total = total + jnp.sum(theirs * theirs, axis=-1, keepdims=True)
            normed = mine * lax.rsqrt(total / D + EPS) * gain_ref[...]
            span = pl.ds(t * requests, requests)
            for head in range(groups * GROUP):
                hid[head, span, :] = mine[:, head * HD : (head + 1) * HD]
                x[head, span, :] = normed[:, head * HD : (head + 1) * HD]
        for g in range(groups):
            for source, target in ((x, kn), (hid, vn)):
                summed = source[g * GROUP]
                for h in range(1, GROUP):
                    summed = summed + source[g * GROUP + h]
                target[g] = summed * (1.0 / GROUP)

        lines = groups * rows
        position = lax.broadcasted_iota(jnp.int32, (lines, blocks * block_tok), 1)
        new_step = lax.broadcasted_iota(jnp.int32, (lines, TILE), 1)
        own_step = lax.rem(lax.broadcasted_iota(jnp.int32, (lines, TILE), 0), steps)
        new_mask = new_step <= own_step
        none = jnp.zeros((rows, HD), jnp.float32)
        blank = jnp.zeros((TILE - steps, kv_width), jnp.float32)

        def newest(source, request):
            every = [source[g, pl.ds(request, steps, stride=requests), :] for g in range(groups)]
            return jnp.concatenate([jnp.concatenate(every, axis=1), blank], axis=0).astype(
                jnp.bfloat16
            )

        fresh[:, pl.ds(0, kv_width)] = newest(kn, handed)
        fresh[:, pl.ds(kv_width, kv_width)] = newest(vn, handed)

        @pl.loop(0, requests)
        def _(r):
            here = pl.ds(r, steps, stride=requests)
            mask = position < lens_ref[instance, r]
            at = [tables_ref[0, r, j] for j in range(blocks)]
            new_k, new_v = newest(kn, r), newest(vn, r)
            old_k, old_v = [
                jnp.concatenate([cache[0, 0, at[j]] for j in range(blocks)], axis=0)
                for cache in (k_ref, v_ref)
            ]
            stripes = []
            for g in range(groups):
                query = [x[g * GROUP + h, here, :] for h in range(GROUP)]
                stripe = [none] * groups
                stripe[g] = jnp.concatenate(query, axis=0)
                stripes.append(jnp.concatenate(stripe, axis=1))
            query = jnp.concatenate(stripes, axis=0).astype(jnp.bfloat16)
            score, score_new = [
                scale
                * lax.dot_general(
                    query, key, (((1,), (1,)), ((), ())), preferred_element_type=jnp.float32
                )
                for key in (old_k, new_k)
            ]
            score = jnp.where(mask, score, -jnp.inf)
            score_new = jnp.where(new_mask, score_new, -jnp.inf)
            top = jnp.maximum(
                jnp.max(score, axis=-1, keepdims=True), jnp.max(score_new, axis=-1, keepdims=True)
            )
            expo = jnp.exp(score - top)
            expo_new = jnp.exp(score_new - top)
            total = jnp.sum(expo, axis=-1, keepdims=True) + jnp.sum(
                expo_new, axis=-1, keepdims=True
            )
            weight = (expo / total).astype(jnp.bfloat16)
            weight_new = (expo_new / total).astype(jnp.bfloat16)
            every = jnp.dot(weight, old_v, preferred_element_type=jnp.float32) + jnp.dot(
                weight_new, new_v, preferred_element_type=jnp.float32
            )
            for g in range(groups):
                attended = every[g * rows : (g + 1) * rows, g * HD : (g + 1) * HD]
                attended = attended * lax.rsqrt(
                    jnp.mean(attended * attended, axis=-1, keepdims=True) + EPS
                )
                for h in range(GROUP):
                    o[g * GROUP + h, here, :] = attended[h * steps : (h + 1) * steps]

        for t in range(steps):
            span = pl.ds(t * requests, requests)
            for head in range(groups * GROUP):
                lanes = pl.ds(head * HD, HD)
                out[0, t, :, lanes] = (
                    hid[head, span, :] + o[head, span, :] * out_gain_ref[:, lanes]
                ).astype(jnp.bfloat16)
        sends = [
            pltpu.make_async_copy(out, out_ref, o_sem.at[0]),
            pltpu.make_async_copy(fresh, fresh_ref, o_sem.at[1]),
        ]
        for copy in sends:
            copy.start()
        for copy in sends:
            copy.wait()


@functools.partial(jax.jit, static_argnums=0)
def layer(
    phase, tables, lens, mig_req, hidden, others, attn_gain, out_gain, k_cache, v_cache, prior
):
    steps, requests, width = hidden.shape
    block_tok, kv_width = k_cache.shape[3:]
    context = tables.shape[2] * block_tok
    lines = steps * requests
    heads = width // HD
    groups = kv_width // HD
    out_shape = (
        jax.ShapeDtypeStruct((1, steps, requests, width), jnp.bfloat16),
        jax.ShapeDtypeStruct((TILE, 2 * kv_width), jnp.bfloat16),
    )
    operands = (tables, lens, mig_req, hidden, attn_gain, out_gain, k_cache, v_cache)
    operands += others + prior
    placed = len(operands) - len(prior)
    return pl.pallas_call(
        functools.partial(layer_kernel, phase, not prior, len(others)),
        out_shape=out_shape,
        in_specs=[SMEM] * 3 + [VMEM] * (5 + len(others)) + [ANY] * len(prior),
        out_specs=(ANY, ANY),
        input_output_aliases={placed + i: i for i in range(len(prior))},
        scratch_shapes=[
            pltpu.VMEM((heads, lines, HD), jnp.float32),
            pltpu.VMEM((heads, lines, HD), jnp.float32),
            pltpu.VMEM((groups, lines, HD), jnp.float32),
            pltpu.VMEM((groups, lines, HD), jnp.float32),
            pltpu.VMEM((heads, lines, HD), jnp.float32),
            pltpu.VMEM((1, steps, requests, width), jnp.bfloat16),
            pltpu.VMEM((TILE, 2 * kv_width), jnp.bfloat16),
            pltpu.SemaphoreType.DMA((2,)),
        ],
        compiler_params=params(32),
        cost_estimate=pl.CostEstimate(
            flops=4 * lines * width * context, bytes_accessed=4 * requests * context * kv_width,
            transcendentals=lines * width * context // HD,
        ),
        name=f"layer_{phase}",
    )(*operands)


def place_kernel(
    lens_ref, mig_ref, partner_ref, first_ref, later_ref, fresh_ref, k_ref, v_ref,
    edge, blank, sems, fetch_sems, store_sems
):
    source = partner_ref[lax.axis_index("inst")]
    length = lens_ref[source, mig_ref[source]]
    context, width = k_ref.shape[2:]
    chunks = context // CHUNK
    border = length // CHUNK
    sides = tuple(enumerate((k_ref, v_ref)))

    early = first_ref.shape[0] // CHUNK

    def rows_of(source, c, side):
        span = pl.ds(pl.multiple_of(c * CHUNK, CHUNK), CHUNK)
        return source.at[span, pl.ds(side * width, width)]

    def fetch(source, c, side):
        return pltpu.make_async_copy(
            rows_of(source, c, side), edge.at[side, pl.ds(0, CHUNK), :], fetch_sems.at[side]
        )

    @pl.when(border < early)
    def _():
        for side, _ in sides:
            fetch(first_ref, jnp.minimum(border, early - 1), side).start()

    @pl.when(border >= early)
    def _():
        for side, _ in sides:
            fetch(later_ref, jnp.clip(border, early, chunks - 1) - early, side).start()

    blank[...] = jnp.zeros_like(blank)

    def move(source, row, c):
        span = pl.ds(pl.multiple_of(c * CHUNK, CHUNK), CHUNK)
        return [
            pltpu.make_async_copy(
                rows_of(source, row, side), target.at[0, 0, span, :], sems.at[side, c]
            )
            for side, target in sides
        ]

    def clears(c):
        span = pl.ds(pl.multiple_of(c * CHUNK, CHUNK), CHUNK)
        return [
            pltpu.make_async_copy(blank, target.at[0, 0, span, :], sems.at[side, c])
            for side, target in sides
        ]

    @pl.loop(0, jnp.minimum(border, early))
    def _(c):
        for copy in move(first_ref, c, c):
            copy.start()

    @pl.loop(early, border)
    def _(c):
        for copy in move(later_ref, c - early, c):
            copy.start()

    @pl.loop(border + 2, chunks)
    def _(c):
        for copy in clears(c):
            copy.start()

    stores = []
    for side, target in sides:
        fetch(first_ref, 0, side).wait()
        place = border * CHUNK + lax.broadcasted_iota(jnp.int32, (2 * CHUNK, width), 0)
        block = jnp.concatenate(
            [edge[side, :CHUNK].astype(jnp.float32), jnp.zeros((CHUNK, width), jnp.float32)], axis=0
        )
        block = jnp.where(place < length, block, 0.0)
        new = fresh_ref[:, pl.ds(side * width, width)].astype(jnp.float32)
        for t in range(STEPS):
            block = jnp.where(place == length + t, new[t : t + 1], block)
        edge[side] = block.astype(jnp.bfloat16)
        for half in range(2):
            stores.append(
                pltpu.make_async_copy(
                    edge.at[side, pl.ds(half * CHUNK, CHUNK), :],
                    target.at[
                        0, 0, pl.ds(jnp.minimum(border + half, chunks - 1) * CHUNK, CHUNK), :
                    ],
                    store_sems.at[side, half],
                )
            )
            if half == 0:
                stores[-1].start()
            else:
                pl.when(border + 1 < chunks)(stores[-1].start)
    for i, store in enumerate(stores):
        if i % 2 == 0:
            store.wait()
        else:
            pl.when(border + 1 < chunks)(store.wait)

    @pl.loop(0, border)
    def _(c):
        for copy in move(first_ref, 0, c):
            copy.wait()

    @pl.loop(border + 2, chunks)
    def _(c):
        for copy in clears(c):
            copy.wait()


@functools.partial(jax.jit, static_argnums=0)
def place(context, lens, mig_req, partner, first, later, fresh):
    width = first.shape[1] // 2
    shape = jax.ShapeDtypeStruct((1, 1, context, width), jnp.bfloat16)
    return pl.pallas_call(
        place_kernel,
        out_shape=(shape, shape),
        in_specs=[SMEM] * 3 + [ANY, ANY, VMEM],
        out_specs=(ANY, ANY),
        scratch_shapes=[
            pltpu.VMEM((2, 2 * CHUNK, width), jnp.bfloat16),
            pltpu.VMEM((CHUNK, width), jnp.bfloat16),
            pltpu.SemaphoreType.DMA((2, context // CHUNK)),
            pltpu.SemaphoreType.DMA((2,)),
            pltpu.SemaphoreType.DMA((2, 2)),
        ],
        compiler_params=params(8),
        name="place",
    )(lens, mig_req, partner, first, later, fresh)


def widen_kernel(got_ref, out_ref, sem):
    copy = pltpu.make_async_copy(got_ref, out_ref.at[pl.ds(0, got_ref.shape[0]), :], sem.at[0])
    copy.start()
    copy.wait()


@functools.partial(jax.jit, static_argnums=0)
def widen(rows, got):
    return pl.pallas_call(
        widen_kernel,
        out_shape=jax.ShapeDtypeStruct((rows, got.shape[1]), got.dtype),
        in_specs=[ANY],
        out_specs=ANY,
        scratch_shapes=[pltpu.SemaphoreType.DMA((1,))],
        compiler_params=params(8),
        name="widen",
    )(got)


def follow(pairs, count):
    def run(handed):
        rows = handed.shape[0]
        if count == 0:
            return handed
        got = lax.ppermute(handed[:count], "inst", pairs)
        return got if count == rows else widen(rows, got)

    return run


@functools.partial(jax.jit, static_argnums=(0, 1))
def gather(start, rows, tables, mig_req, k_cache, v_cache):
    kv_width = k_cache.shape[4]
    return pl.pallas_call(
        functools.partial(gather_kernel, start, rows),
        out_shape=jax.ShapeDtypeStruct((rows, 2 * kv_width), jnp.bfloat16),
        in_specs=[SMEM, SMEM, ANY, ANY],
        out_specs=ANY,
        scratch_shapes=[pltpu.SemaphoreType.DMA((2, rows // CHUNK))],
        compiler_params=params(8),
        name="gather",
    )(tables, mig_req, k_cache, v_cache)


def branch(offset, counts, context):
    def run(emb, attn_gain, out_gain, k_cache, v_cache, tables, lens, partner, mig_req):
        sections = lax.axis_size("section")
        tp = lax.axis_size("tp")
        pairs = [(i, i ^ offset) for i in range(lax.axis_size("inst"))]
        early = counts[0] if len(counts) > 1 else -(-context // (3 * CHUNK)) * CHUNK
        rest = context - early
        handed = gather(0, early, tables, mig_req, k_cache, v_cache)
        first = lax.ppermute(handed, "inst", pairs)
        handed = gather(early, rest, tables, mig_req, k_cache, v_cache)
        if len(counts) == 1:
            later = lax.ppermute(handed, "inst", pairs)

        hidden, prior = emb, ()
        for phase in range(sections):
            if phase > 0:
                hidden = lax.ppermute(prior[0], "section", [(phase - 1, phase)])[0]
            others = tuple(
                lax.ppermute(hidden, "tp", [(i, (i + by) % tp) for i in range(tp)])
                for by in range(1, tp)
            )
            prior = tuple(
                layer(
                    phase, tables, lens, mig_req, hidden, others, attn_gain, out_gain,
                    k_cache, v_cache, prior,
                )
            )
        fresh = lax.ppermute(prior[1], "inst", pairs)
        if len(counts) > 1:
            handed, _ = lax.optimization_barrier((handed, prior[1]))
            later = lax.switch(
                pick(tuple(counts), lens, mig_req, partner),
                [follow(pairs, count - early) for count in counts],
                handed,
            )
        arrived = place(context, lens, mig_req, partner, first, later, fresh)
        return (prior[0], arrived[0], arrived[1])

    return run


def local(emb, attn_gain, out_gain, k_cache, v_cache, tables, lens, partner, mig_req):
    instances, sections = lax.axis_size("inst"), lax.axis_size("section")
    context = tables.shape[2] * k_cache.shape[3]
    branches = [
        branch(offset, row_counts(offset, instances, sections, context), context)
        for offset in range(1, instances)
    ]
    return lax.switch(
        partner[0] - 1, branches, emb, attn_gain, out_gain, k_cache, v_cache, tables, lens,
        partner, mig_req,
    )


def solution(mesh):
    return jax.shard_map(
        local,
        mesh=mesh,
        in_specs=(
            P(None, ("groups", "inst"), "tp"),
            P("section", "tp"),
            P("section", "tp"),
            P(("groups", "inst"), "section", None, None, "tp"),
            P(("groups", "inst"), "section", None, None, "tp"),
            P(("groups", "inst"), None, None),
            P("groups", None),
            P(),
            P("groups"),
        ),
        out_specs=(
            P("section", None, ("groups", "inst"), "tp"),
            P(("groups", "inst"), "section", None, "tp"),
            P(("groups", "inst"), "section", None, "tp"),
        ),
        check_vma=False,
    )
```

```python
import functools

import jax
import jax.numpy as jnp
from jax import lax
from jax.experimental import pallas as pl
from jax.experimental.pallas import tpu as pltpu
from jax.sharding import PartitionSpec as P

QH = 64
KVH = 8
HD = 128
D = 8192
GROUP = QH // KVH
TILE = 16
CHUNK = 64
STEPS = 4
FINE = 32
EPS = 1e-05

SMEM = pl.BlockSpec(memory_space=pltpu.SMEM)
VMEM = pl.BlockSpec(memory_space=pltpu.VMEM)
ANY = pl.BlockSpec(memory_space=pl.ANY)


def params(mib):
    return pltpu.CompilerParams(vmem_limit_bytes=mib << 20)


def row_counts(offset, instances, sections, context):
    crossing = max(
        sum(1 for i in range(instances) if i <= cut < i ^ offset) for cut in range(instances)
    )
    if instances * sections > 8:
        shares = (24,)
    elif crossing == 1:
        shares = (18, 20, 22, 24)
    else:
        shares = (10, 12, 14) + tuple(range(16, 25))
    counts = {min(context, -(-context * share // (24 * FINE)) * FINE) for share in shares}
    lowest = min(counts)
    return sorted({-(-lowest // CHUNK) * CHUNK} | (counts - {lowest}))


def pick_kernel(counts, lens_ref, mig_ref, partner_ref, choice_ref):
    instance = lax.axis_index("inst")
    other = partner_ref[instance]
    longest = jnp.maximum(
        lens_ref[instance, mig_ref[instance]], lens_ref[other, mig_ref[other]]
    )
    choice = jnp.int32(0)
    for count in counts[:-1]:
        choice = choice + jnp.where(longest > count, 1, 0)
    choice_ref[0] = choice


@functools.partial(jax.jit, static_argnums=0)
def pick(counts, lens, mig_req, partner):
    return pl.pallas_call(
        functools.partial(pick_kernel, counts),
        out_shape=jax.ShapeDtypeStruct((1,), jnp.int32),
        in_specs=[SMEM] * 3,
        out_specs=SMEM,
        name="pick",
    )(lens, mig_req, partner)[0]


def gather_kernel(start, rows, tables_ref, mig_ref, k_ref, v_ref, out_ref, sems):
    request = mig_ref[lax.axis_index("inst")]
    block_tok, width = k_ref.shape[3:]
    parts = block_tok // CHUNK

    def copies(c):
        at = c + start // CHUNK
        block = tables_ref[0, request, lax.div(at, parts)]
        span = pl.ds(pl.multiple_of(lax.rem(at, parts) * CHUNK, CHUNK), CHUNK)
        place = pl.ds(pl.multiple_of(c * CHUNK, CHUNK), CHUNK)
        return [
            pltpu.make_async_copy(
                cache.at[0, 0, block, span, :],
                out_ref.at[place, pl.ds(side * width, width)],
                sems.at[side, c],
            )
            for side, cache in enumerate((k_ref, v_ref))
        ]

    @pl.loop(0, rows // CHUNK)
    def _(c):
        for copy in copies(c):
            copy.start()

    @pl.loop(0, rows // CHUNK)
    def _(c):
        for copy in copies(c):
            copy.wait()


def layer_kernel(
    phase, first, peers, tables_ref, lens_ref, mig_ref, hid_ref, gain_ref, out_gain_ref,
    k_ref, v_ref, *rest
):
    other_refs, rest = rest[:peers], rest[peers:]
    if not first:
        rest = rest[2:]
    out_ref, fresh_ref, hid, x, kn, vn, o, out, fresh, o_sem = rest
    steps, requests, width = hid_ref.shape
    block_tok, kv_width = k_ref.shape[3:]
    blocks = tables_ref.shape[2]
    groups = kv_width // HD
    rows = GROUP * steps
    scale = HD ** (-0.5)

    @pl.when(lax.axis_index("section") == phase)
    def _():
        instance = lax.axis_index("inst")
        handed = mig_ref[instance]
        for t in range(steps):
            mine = hid_ref[t].astype(jnp.float32)
            total = jnp.sum(mine * mine, axis=-1, keepdims=True)
            for other_ref in other_refs:
                theirs = other_ref[t].astype(jnp.float32)
                total = total + jnp.sum(theirs * theirs, axis=-1, keepdims=True)
            normed = mine * lax.rsqrt(total / D + EPS) * gain_ref[...]
            span = pl.ds(t * requests, requests)
            for head in range(groups * GROUP):
                hid[head, span, :] = mine[:, head * HD : (head + 1) * HD]
                x[head, span, :] = normed[:, head * HD : (head + 1) * HD]
        for g in range(groups):
            for source, target in ((x, kn), (hid, vn)):
                summed = source[g * GROUP]
                for h in range(1, GROUP):
                    summed = summed + source[g * GROUP + h]
                target[g] = summed * (1.0 / GROUP)

        lines = groups * rows
        position = lax.broadcasted_iota(jnp.int32, (lines, blocks * block_tok), 1)
        new_step = lax.broadcasted_iota(jnp.int32, (lines, TILE), 1)
        own_step = lax.rem(lax.broadcasted_iota(jnp.int32, (lines, TILE), 0), steps)
        new_mask = new_step <= own_step
        none = jnp.zeros((rows, HD), jnp.float32)
        blank = jnp.zeros((TILE - steps, kv_width), jnp.float32)

        def newest(source, request):
            every = [source[g, pl.ds(request, steps, stride=requests), :] for g in range(groups)]
            return jnp.concatenate([jnp.concatenate(every, axis=1), blank], axis=0).astype(
                jnp.bfloat16
            )

        fresh[:, pl.ds(0, kv_width)] = newest(kn, handed)
        fresh[:, pl.ds(kv_width, kv_width)] = newest(vn, handed)

        @pl.loop(0, requests)
        def _(r):
            here = pl.ds(r, steps, stride=requests)
            mask = position < lens_ref[instance, r]
            at = [tables_ref[0, r, j] for j in range(blocks)]
            new_k, new_v = newest(kn, r), newest(vn, r)
            old_k, old_v = [
                jnp.concatenate([cache[0, 0, at[j]] for j in range(blocks)], axis=0)
                for cache in (k_ref, v_ref)
            ]
            stripes = []
            for g in range(groups):
                query = [x[g * GROUP + h, here, :] for h in range(GROUP)]
                stripe = [none] * groups
                stripe[g] = jnp.concatenate(query, axis=0)
                stripes.append(jnp.concatenate(stripe, axis=1))
            query = jnp.concatenate(stripes, axis=0).astype(jnp.bfloat16)
            score, score_new = [
                scale
                * lax.dot_general(
                    query, key, (((1,), (1,)), ((), ())), preferred_element_type=jnp.float32
                )
                for key in (old_k, new_k)
            ]
            score = jnp.where(mask, score, -jnp.inf)
            score_new = jnp.where(new_mask, score_new, -jnp.inf)
            top = jnp.maximum(
                jnp.max(score, axis=-1, keepdims=True), jnp.max(score_new, axis=-1, keepdims=True)
            )
            expo = jnp.exp(score - top)
            expo_new = jnp.exp(score_new - top)
            total = jnp.sum(expo, axis=-1, keepdims=True) + jnp.sum(
                expo_new, axis=-1, keepdims=True
            )
            weight = (expo / total).astype(jnp.bfloat16)
            weight_new = (expo_new / total).astype(jnp.bfloat16)
            every = jnp.dot(weight, old_v, preferred_element_type=jnp.float32) + jnp.dot(
                weight_new, new_v, preferred_element_type=jnp.float32
            )
            for g in range(groups):
                attended = every[g * rows : (g + 1) * rows, g * HD : (g + 1) * HD]
                attended = attended * lax.rsqrt(
                    jnp.mean(attended * attended, axis=-1, keepdims=True) + EPS
                )
                for h in range(GROUP):
                    o[g * GROUP + h, here, :] = attended[h * steps : (h + 1) * steps]

        for t in range(steps):
            span = pl.ds(t * requests, requests)
            for head in range(groups * GROUP):
                lanes = pl.ds(head * HD, HD)
                out[0, t, :, lanes] = (
                    hid[head, span, :] + o[head, span, :] * out_gain_ref[:, lanes]
                ).astype(jnp.bfloat16)
        sends = [
            pltpu.make_async_copy(out, out_ref, o_sem.at[0]),
            pltpu.make_async_copy(fresh, fresh_ref, o_sem.at[1]),
        ]
        for copy in sends:
            copy.start()
        for copy in sends:
            copy.wait()


@functools.partial(jax.jit, static_argnums=0)
def layer(
    phase, tables, lens, mig_req, hidden, others, attn_gain, out_gain, k_cache, v_cache, prior
):
    steps, requests, width = hidden.shape
    block_tok, kv_width = k_cache.shape[3:]
    context = tables.shape[2] * block_tok
    lines = steps * requests
    heads = width // HD
    groups = kv_width // HD
    out_shape = (
        jax.ShapeDtypeStruct((1, steps, requests, width), jnp.bfloat16),
        jax.ShapeDtypeStruct((TILE, 2 * kv_width), jnp.bfloat16),
    )
    operands = (tables, lens, mig_req, hidden, attn_gain, out_gain, k_cache, v_cache)
    operands += others + prior
    placed = len(operands) - len(prior)
    return pl.pallas_call(
        functools.partial(layer_kernel, phase, not prior, len(others)),
        out_shape=out_shape,
        in_specs=[SMEM] * 3 + [VMEM] * (5 + len(others)) + [ANY] * len(prior),
        out_specs=(ANY, ANY),
        input_output_aliases={placed + i: i for i in range(len(prior))},
        scratch_shapes=[
            pltpu.VMEM((heads, lines, HD), jnp.float32),
            pltpu.VMEM((heads, lines, HD), jnp.float32),
            pltpu.VMEM((groups, lines, HD), jnp.float32),
            pltpu.VMEM((groups, lines, HD), jnp.float32),
            pltpu.VMEM((heads, lines, HD), jnp.float32),
            pltpu.VMEM((1, steps, requests, width), jnp.bfloat16),
            pltpu.VMEM((TILE, 2 * kv_width), jnp.bfloat16),
            pltpu.SemaphoreType.DMA((2,)),
        ],
        compiler_params=params(32),
        cost_estimate=pl.CostEstimate(
            flops=4 * lines * width * context, bytes_accessed=4 * requests * context * kv_width,
            transcendentals=lines * width * context // HD,
        ),
        name=f"layer_{phase}",
    )(*operands)


def place_kernel(
    lens_ref, mig_ref, partner_ref, first_ref, later_ref, fresh_ref, k_ref, v_ref,
    edge, blank, sems, fetch_sems, store_sems
):
    source = partner_ref[lax.axis_index("inst")]
    length = lens_ref[source, mig_ref[source]]
    context, width = k_ref.shape[2:]
    chunks = context // CHUNK
    border = length // CHUNK
    sides = tuple(enumerate((k_ref, v_ref)))

    early = first_ref.shape[0] // CHUNK

    def rows_of(source, c, side):
        span = pl.ds(pl.multiple_of(c * CHUNK, CHUNK), CHUNK)
        return source.at[span, pl.ds(side * width, width)]

    def fetch(source, c, side):
        return pltpu.make_async_copy(
            rows_of(source, c, side), edge.at[side, pl.ds(0, CHUNK), :], fetch_sems.at[side]
        )

    @pl.when(border < early)
    def _():
        for side, _ in sides:
            fetch(first_ref, jnp.minimum(border, early - 1), side).start()

    @pl.when(border >= early)
    def _():
        for side, _ in sides:
            fetch(later_ref, jnp.clip(border, early, chunks - 1) - early, side).start()

    blank[...] = jnp.zeros_like(blank)

    def move(source, row, c):
        span = pl.ds(pl.multiple_of(c * CHUNK, CHUNK), CHUNK)
        return [
            pltpu.make_async_copy(
                rows_of(source, row, side), target.at[0, 0, span, :], sems.at[side, c]
            )
            for side, target in sides
        ]

    def clears(c):
        span = pl.ds(pl.multiple_of(c * CHUNK, CHUNK), CHUNK)
        return [
            pltpu.make_async_copy(blank, target.at[0, 0, span, :], sems.at[side, c])
            for side, target in sides
        ]

    @pl.loop(0, jnp.minimum(border, early))
    def _(c):
        for copy in move(first_ref, c, c):
            copy.start()

    @pl.loop(early, border)
    def _(c):
        for copy in move(later_ref, c - early, c):
            copy.start()

    @pl.loop(border + 2, chunks)
    def _(c):
        for copy in clears(c):
            copy.start()

    stores = []
    for side, target in sides:
        fetch(first_ref, 0, side).wait()
        place = border * CHUNK + lax.broadcasted_iota(jnp.int32, (2 * CHUNK, width), 0)
        block = jnp.concatenate(
            [edge[side, :CHUNK].astype(jnp.float32), jnp.zeros((CHUNK, width), jnp.float32)], axis=0
        )
        block = jnp.where(place < length, block, 0.0)
        new = fresh_ref[:, pl.ds(side * width, width)].astype(jnp.float32)
        for t in range(STEPS):
            block = jnp.where(place == length + t, new[t : t + 1], block)
        edge[side] = block.astype(jnp.bfloat16)
        for half in range(2):
            stores.append(
                pltpu.make_async_copy(
                    edge.at[side, pl.ds(half * CHUNK, CHUNK), :],
                    target.at[
                        0, 0, pl.ds(jnp.minimum(border + half, chunks - 1) * CHUNK, CHUNK), :
                    ],
                    store_sems.at[side, half],
                )
            )
            if half == 0:
                stores[-1].start()
            else:
                pl.when(border + 1 < chunks)(stores[-1].start)
    for i, store in enumerate(stores):
        if i % 2 == 0:
            store.wait()
        else:
            pl.when(border + 1 < chunks)(store.wait)

    @pl.loop(0, border)
    def _(c):
        for copy in move(first_ref, 0, c):
            copy.wait()

    @pl.loop(border + 2, chunks)
    def _(c):
        for copy in clears(c):
            copy.wait()


@functools.partial(jax.jit, static_argnums=0)
def place(context, lens, mig_req, partner, first, later, fresh):
    width = first.shape[1] // 2
    shape = jax.ShapeDtypeStruct((1, 1, context, width), jnp.bfloat16)
    return pl.pallas_call(
        place_kernel,
        out_shape=(shape, shape),
        in_specs=[SMEM] * 3 + [ANY, ANY, VMEM],
        out_specs=(ANY, ANY),
        scratch_shapes=[
            pltpu.VMEM((2, 2 * CHUNK, width), jnp.bfloat16),
            pltpu.VMEM((CHUNK, width), jnp.bfloat16),
            pltpu.SemaphoreType.DMA((2, context // CHUNK)),
            pltpu.SemaphoreType.DMA((2,)),
            pltpu.SemaphoreType.DMA((2, 2)),
        ],
        compiler_params=params(8),
        name="place",
    )(lens, mig_req, partner, first, later, fresh)


def widen_kernel(got_ref, out_ref, sem):
    copy = pltpu.make_async_copy(got_ref, out_ref.at[pl.ds(0, got_ref.shape[0]), :], sem.at[0])
    copy.start()
    copy.wait()


@functools.partial(jax.jit, static_argnums=0)
def widen(rows, got):
    return pl.pallas_call(
        widen_kernel,
        out_shape=jax.ShapeDtypeStruct((rows, got.shape[1]), got.dtype),
        in_specs=[ANY],
        out_specs=ANY,
        scratch_shapes=[pltpu.SemaphoreType.DMA((1,))],
        compiler_params=params(8),
        name="widen",
    )(got)


def follow(pairs, count):
    def run(handed):
        rows = handed.shape[0]
        if count == 0:
            return handed
        got = lax.ppermute(handed[:count], "inst", pairs)
        return got if count == rows else widen(rows, got)

    return run


@functools.partial(jax.jit, static_argnums=(0, 1))
def gather(start, rows, tables, mig_req, k_cache, v_cache):
    kv_width = k_cache.shape[4]
    return pl.pallas_call(
        functools.partial(gather_kernel, start, rows),
        out_shape=jax.ShapeDtypeStruct((rows, 2 * kv_width), jnp.bfloat16),
        in_specs=[SMEM, SMEM, ANY, ANY],
        out_specs=ANY,
        scratch_shapes=[pltpu.SemaphoreType.DMA((2, rows // CHUNK))],
        compiler_params=params(8),
        name="gather",
    )(tables, mig_req, k_cache, v_cache)


def branch(offset, counts, context):
    def run(emb, attn_gain, out_gain, k_cache, v_cache, tables, lens, partner, mig_req):
        sections = lax.axis_size("section")
        tp = lax.axis_size("tp")
        pairs = [(i, i ^ offset) for i in range(lax.axis_size("inst"))]
        early = counts[0] if len(counts) > 1 else -(-context // (3 * CHUNK)) * CHUNK
        rest = context - early
        handed = gather(0, early, tables, mig_req, k_cache, v_cache)
        first = lax.ppermute(handed, "inst", pairs)
        handed = gather(early, rest, tables, mig_req, k_cache, v_cache)
        if len(counts) == 1:
            later = lax.ppermute(handed, "inst", pairs)

        hidden, prior = emb, ()
        for phase in range(sections):
            if phase > 0:
                hidden = lax.ppermute(prior[0], "section", [(phase - 1, phase)])[0]
            others = tuple(
                lax.ppermute(hidden, "tp", [(i, (i + by) % tp) for i in range(tp)])
                for by in range(1, tp)
            )
            prior = tuple(
                layer(
                    phase, tables, lens, mig_req, hidden, others, attn_gain, out_gain,
                    k_cache, v_cache, prior,
                )
            )
        fresh = lax.ppermute(prior[1], "inst", pairs)
        if len(counts) > 1:
            handed, _ = lax.optimization_barrier((handed, prior[1]))
            later = lax.switch(
                pick(tuple(counts), lens, mig_req, partner),
                [follow(pairs, count - early) for count in counts],
                handed,
            )
        arrived = place(context, lens, mig_req, partner, first, later, fresh)
        return (prior[0], arrived[0], arrived[1])

    return run


def local(emb, attn_gain, out_gain, k_cache, v_cache, tables, lens, partner, mig_req):
    instances, sections = lax.axis_size("inst"), lax.axis_size("section")
    context = tables.shape[2] * k_cache.shape[3]
    branches = [
        branch(offset, row_counts(offset, instances, sections, context), context)
        for offset in range(1, instances)
    ]
    return lax.switch(
        partner[0] - 1, branches, emb, attn_gain, out_gain, k_cache, v_cache, tables, lens,
        partner, mig_req,
    )


def solution(mesh):
    return jax.shard_map(
        local,
        mesh=mesh,
        in_specs=(
            P(None, ("groups", "inst"), "tp"),
            P("section", "tp"),
            P("section", "tp"),
            P(("groups", "inst"), "section", None, None, "tp"),
            P(("groups", "inst"), "section", None, None, "tp"),
            P(("groups", "inst"), None, None),
            P("groups", None),
            P(),
            P("groups"),
        ),
        out_specs=(
            P("section", None, ("groups", "inst"), "tp"),
            P(("groups", "inst"), "section", None, "tp"),
            P(("groups", "inst"), "section", None, "tp"),
        ),
        check_vma=False,
    )
```

```python
import functools

import jax
import jax.numpy as jnp
from jax import lax
from jax.experimental import pallas as pl
from jax.experimental.pallas import tpu as pltpu
from jax.sharding import PartitionSpec as P

QH = 64
KVH = 8
HD = 128
D = 8192
GROUP = QH // KVH
TILE = 16
CHUNK = 64
STEPS = 4
FINE = 32
EPS = 1e-05

SMEM = pl.BlockSpec(memory_space=pltpu.SMEM)
VMEM = pl.BlockSpec(memory_space=pltpu.VMEM)
ANY = pl.BlockSpec(memory_space=pl.ANY)


def params(mib):
    return pltpu.CompilerParams(vmem_limit_bytes=mib << 20)


def row_counts(offset, instances, sections, context):
    crossing = max(
        sum(1 for i in range(instances) if i <= cut < i ^ offset) for cut in range(instances)
    )
    if instances * sections > 8:
        shares = (24,)
    elif crossing == 1:
        shares = tuple(range(18, 25))
    else:
        shares = (10, 12, 14) + tuple(range(16, 25))
    counts = {min(context, -(-context * share // (24 * FINE)) * FINE) for share in shares}
    lowest = min(counts)
    return sorted({-(-lowest // CHUNK) * CHUNK} | (counts - {lowest}))


def pick_kernel(counts, lens_ref, mig_ref, partner_ref, choice_ref):
    instance = lax.axis_index("inst")
    other = partner_ref[instance]
    longest = jnp.maximum(
        lens_ref[instance, mig_ref[instance]], lens_ref[other, mig_ref[other]]
    )
    choice = jnp.int32(0)
    for count in counts[:-1]:
        choice = choice + jnp.where(longest > count, 1, 0)
    choice_ref[0] = choice


@functools.partial(jax.jit, static_argnums=0)
def pick(counts, lens, mig_req, partner):
    return pl.pallas_call(
        functools.partial(pick_kernel, counts),
        out_shape=jax.ShapeDtypeStruct((1,), jnp.int32),
        in_specs=[SMEM] * 3,
        out_specs=SMEM,
        name="pick",
    )(lens, mig_req, partner)[0]


def gather_kernel(start, rows, tables_ref, mig_ref, k_ref, v_ref, out_ref, sems):
    request = mig_ref[lax.axis_index("inst")]
    block_tok, width = k_ref.shape[3:]
    parts = block_tok // CHUNK

    def copies(c):
        at = c + start // CHUNK
        block = tables_ref[0, request, lax.div(at, parts)]
        span = pl.ds(pl.multiple_of(lax.rem(at, parts) * CHUNK, CHUNK), CHUNK)
        place = pl.ds(pl.multiple_of(c * CHUNK, CHUNK), CHUNK)
        return [
            pltpu.make_async_copy(
                cache.at[0, 0, block, span, :],
                out_ref.at[place, pl.ds(side * width, width)],
                sems.at[side, c],
            )
            for side, cache in enumerate((k_ref, v_ref))
        ]

    @pl.loop(0, rows // CHUNK)
    def _(c):
        for copy in copies(c):
            copy.start()

    @pl.loop(0, rows // CHUNK)
    def _(c):
        for copy in copies(c):
            copy.wait()


def layer_kernel(
    phase, first, peers, tables_ref, lens_ref, mig_ref, hid_ref, gain_ref, out_gain_ref,
    k_ref, v_ref, *rest
):
    other_refs, rest = rest[:peers], rest[peers:]
    if not first:
        rest = rest[2:]
    out_ref, fresh_ref, hid, x, kn, vn, o, out, fresh, o_sem = rest
    steps, requests, width = hid_ref.shape
    block_tok, kv_width = k_ref.shape[3:]
    blocks = tables_ref.shape[2]
    groups = kv_width // HD
    rows = GROUP * steps
    scale = HD ** (-0.5)

    @pl.when(lax.axis_index("section") == phase)
    def _():
        instance = lax.axis_index("inst")
        handed = mig_ref[instance]
        for t in range(steps):
            mine = hid_ref[t].astype(jnp.float32)
            total = jnp.sum(mine * mine, axis=-1, keepdims=True)
            for other_ref in other_refs:
                theirs = other_ref[t].astype(jnp.float32)
                total = total + jnp.sum(theirs * theirs, axis=-1, keepdims=True)
            normed = mine * lax.rsqrt(total / D + EPS) * gain_ref[...]
            span = pl.ds(t * requests, requests)
            for head in range(groups * GROUP):
                hid[head, span, :] = mine[:, head * HD : (head + 1) * HD]
                x[head, span, :] = normed[:, head * HD : (head + 1) * HD]
        for g in range(groups):
            for source, target in ((x, kn), (hid, vn)):
                summed = source[g * GROUP]
                for h in range(1, GROUP):
                    summed = summed + source[g * GROUP + h]
                target[g] = summed * (1.0 / GROUP)

        lines = groups * rows
        position = lax.broadcasted_iota(jnp.int32, (lines, blocks * block_tok), 1)
        new_step = lax.broadcasted_iota(jnp.int32, (lines, TILE), 1)
        own_step = lax.rem(lax.broadcasted_iota(jnp.int32, (lines, TILE), 0), steps)
        new_mask = new_step <= own_step
        none = jnp.zeros((rows, HD), jnp.float32)
        blank = jnp.zeros((TILE - steps, kv_width), jnp.float32)

        def newest(source, request):
            every = [source[g, pl.ds(request, steps, stride=requests), :] for g in range(groups)]
            return jnp.concatenate([jnp.concatenate(every, axis=1), blank], axis=0).astype(
                jnp.bfloat16
            )

        fresh[:, pl.ds(0, kv_width)] = newest(kn, handed)
        fresh[:, pl.ds(kv_width, kv_width)] = newest(vn, handed)

        @pl.loop(0, requests)
        def _(r):
            here = pl.ds(r, steps, stride=requests)
            mask = position < lens_ref[instance, r]
            at = [tables_ref[0, r, j] for j in range(blocks)]
            new_k, new_v = newest(kn, r), newest(vn, r)
            old_k, old_v = [
                jnp.concatenate([cache[0, 0, at[j]] for j in range(blocks)], axis=0)
                for cache in (k_ref, v_ref)
            ]
            stripes = []
            for g in range(groups):
                query = [x[g * GROUP + h, here, :] for h in range(GROUP)]
                stripe = [none] * groups
                stripe[g] = jnp.concatenate(query, axis=0)
                stripes.append(jnp.concatenate(stripe, axis=1))
            query = jnp.concatenate(stripes, axis=0).astype(jnp.bfloat16)
            score, score_new = [
                scale
                * lax.dot_general(
                    query, key, (((1,), (1,)), ((), ())), preferred_element_type=jnp.float32
                )
                for key in (old_k, new_k)
            ]
            score = jnp.where(mask, score, -jnp.inf)
            score_new = jnp.where(new_mask, score_new, -jnp.inf)
            top = jnp.maximum(
                jnp.max(score, axis=-1, keepdims=True), jnp.max(score_new, axis=-1, keepdims=True)
            )
            expo = jnp.exp(score - top)
            expo_new = jnp.exp(score_new - top)
            total = jnp.sum(expo, axis=-1, keepdims=True) + jnp.sum(
                expo_new, axis=-1, keepdims=True
            )
            weight = (expo / total).astype(jnp.bfloat16)
            weight_new = (expo_new / total).astype(jnp.bfloat16)
            every = jnp.dot(weight, old_v, preferred_element_type=jnp.float32) + jnp.dot(
                weight_new, new_v, preferred_element_type=jnp.float32
            )
            for g in range(groups):
                attended = every[g * rows : (g + 1) * rows, g * HD : (g + 1) * HD]
                attended = attended * lax.rsqrt(
                    jnp.mean(attended * attended, axis=-1, keepdims=True) + EPS
                )
                for h in range(GROUP):
                    o[g * GROUP + h, here, :] = attended[h * steps : (h + 1) * steps]

        for t in range(steps):
            span = pl.ds(t * requests, requests)
            for head in range(groups * GROUP):
                lanes = pl.ds(head * HD, HD)
                out[0, t, :, lanes] = (
                    hid[head, span, :] + o[head, span, :] * out_gain_ref[:, lanes]
                ).astype(jnp.bfloat16)
        sends = [
            pltpu.make_async_copy(out, out_ref, o_sem.at[0]),
            pltpu.make_async_copy(fresh, fresh_ref, o_sem.at[1]),
        ]
        for copy in sends:
            copy.start()
        for copy in sends:
            copy.wait()


@functools.partial(jax.jit, static_argnums=0)
def layer(
    phase, tables, lens, mig_req, hidden, others, attn_gain, out_gain, k_cache, v_cache, prior
):
    steps, requests, width = hidden.shape
    block_tok, kv_width = k_cache.shape[3:]
    context = tables.shape[2] * block_tok
    lines = steps * requests
    heads = width // HD
    groups = kv_width // HD
    out_shape = (
        jax.ShapeDtypeStruct((1, steps, requests, width), jnp.bfloat16),
        jax.ShapeDtypeStruct((TILE, 2 * kv_width), jnp.bfloat16),
    )
    operands = (tables, lens, mig_req, hidden, attn_gain, out_gain, k_cache, v_cache)
    operands += others + prior
    placed = len(operands) - len(prior)
    return pl.pallas_call(
        functools.partial(layer_kernel, phase, not prior, len(others)),
        out_shape=out_shape,
        in_specs=[SMEM] * 3 + [VMEM] * (5 + len(others)) + [ANY] * len(prior),
        out_specs=(ANY, ANY),
        input_output_aliases={placed + i: i for i in range(len(prior))},
        scratch_shapes=[
            pltpu.VMEM((heads, lines, HD), jnp.float32),
            pltpu.VMEM((heads, lines, HD), jnp.float32),
            pltpu.VMEM((groups, lines, HD), jnp.float32),
            pltpu.VMEM((groups, lines, HD), jnp.float32),
            pltpu.VMEM((heads, lines, HD), jnp.float32),
            pltpu.VMEM((1, steps, requests, width), jnp.bfloat16),
            pltpu.VMEM((TILE, 2 * kv_width), jnp.bfloat16),
            pltpu.SemaphoreType.DMA((2,)),
        ],
        compiler_params=params(32),
        cost_estimate=pl.CostEstimate(
            flops=4 * lines * width * context, bytes_accessed=4 * requests * context * kv_width,
            transcendentals=lines * width * context // HD,
        ),
        name=f"layer_{phase}",
    )(*operands)


def place_kernel(
    lens_ref, mig_ref, partner_ref, first_ref, later_ref, fresh_ref, k_ref, v_ref,
    edge, blank, sems, fetch_sems, store_sems
):
    source = partner_ref[lax.axis_index("inst")]
    length = lens_ref[source, mig_ref[source]]
    context, width = k_ref.shape[2:]
    chunks = context // CHUNK
    border = length // CHUNK
    sides = tuple(enumerate((k_ref, v_ref)))

    early = first_ref.shape[0] // CHUNK

    def rows_of(source, c, side):
        span = pl.ds(pl.multiple_of(c * CHUNK, CHUNK), CHUNK)
        return source.at[span, pl.ds(side * width, width)]

    def fetch(source, c, side):
        return pltpu.make_async_copy(
            rows_of(source, c, side), edge.at[side, pl.ds(0, CHUNK), :], fetch_sems.at[side]
        )

    @pl.when(border < early)
    def _():
        for side, _ in sides:
            fetch(first_ref, jnp.minimum(border, early - 1), side).start()

    @pl.when(border >= early)
    def _():
        for side, _ in sides:
            fetch(later_ref, jnp.clip(border, early, chunks - 1) - early, side).start()

    blank[...] = jnp.zeros_like(blank)

    def move(source, row, c):
        span = pl.ds(pl.multiple_of(c * CHUNK, CHUNK), CHUNK)
        return [
            pltpu.make_async_copy(
                rows_of(source, row, side), target.at[0, 0, span, :], sems.at[side, c]
            )
            for side, target in sides
        ]

    def clears(c):
        span = pl.ds(pl.multiple_of(c * CHUNK, CHUNK), CHUNK)
        return [
            pltpu.make_async_copy(blank, target.at[0, 0, span, :], sems.at[side, c])
            for side, target in sides
        ]

    @pl.loop(0, jnp.minimum(border, early))
    def _(c):
        for copy in move(first_ref, c, c):
            copy.start()

    @pl.loop(early, border)
    def _(c):
        for copy in move(later_ref, c - early, c):
            copy.start()

    @pl.loop(border + 2, chunks)
    def _(c):
        for copy in clears(c):
            copy.start()

    stores = []
    for side, target in sides:
        fetch(first_ref, 0, side).wait()
        place = border * CHUNK + lax.broadcasted_iota(jnp.int32, (2 * CHUNK, width), 0)
        block = jnp.concatenate(
            [edge[side, :CHUNK].astype(jnp.float32), jnp.zeros((CHUNK, width), jnp.float32)], axis=0
        )
        block = jnp.where(place < length, block, 0.0)
        new = fresh_ref[:, pl.ds(side * width, width)].astype(jnp.float32)
        for t in range(STEPS):
            block = jnp.where(place == length + t, new[t : t + 1], block)
        edge[side] = block.astype(jnp.bfloat16)
        for half in range(2):
            stores.append(
                pltpu.make_async_copy(
                    edge.at[side, pl.ds(half * CHUNK, CHUNK), :],
                    target.at[
                        0, 0, pl.ds(jnp.minimum(border + half, chunks - 1) * CHUNK, CHUNK), :
                    ],
                    store_sems.at[side, half],
                )
            )
            if half == 0:
                stores[-1].start()
            else:
                pl.when(border + 1 < chunks)(stores[-1].start)
    for i, store in enumerate(stores):
        if i % 2 == 0:
            store.wait()
        else:
            pl.when(border + 1 < chunks)(store.wait)

    @pl.loop(0, border)
    def _(c):
        for copy in move(first_ref, 0, c):
            copy.wait()

    @pl.loop(border + 2, chunks)
    def _(c):
        for copy in clears(c):
            copy.wait()


@functools.partial(jax.jit, static_argnums=0)
def place(context, lens, mig_req, partner, first, later, fresh):
    width = first.shape[1] // 2
    shape = jax.ShapeDtypeStruct((1, 1, context, width), jnp.bfloat16)
    return pl.pallas_call(
        place_kernel,
        out_shape=(shape, shape),
        in_specs=[SMEM] * 3 + [ANY, ANY, VMEM],
        out_specs=(ANY, ANY),
        scratch_shapes=[
            pltpu.VMEM((2, 2 * CHUNK, width), jnp.bfloat16),
            pltpu.VMEM((CHUNK, width), jnp.bfloat16),
            pltpu.SemaphoreType.DMA((2, context // CHUNK)),
            pltpu.SemaphoreType.DMA((2,)),
            pltpu.SemaphoreType.DMA((2, 2)),
        ],
        compiler_params=params(8),
        name="place",
    )(lens, mig_req, partner, first, later, fresh)


def widen_kernel(got_ref, out_ref, sem):
    copy = pltpu.make_async_copy(got_ref, out_ref.at[pl.ds(0, got_ref.shape[0]), :], sem.at[0])
    copy.start()
    copy.wait()


@functools.partial(jax.jit, static_argnums=0)
def widen(rows, got):
    return pl.pallas_call(
        widen_kernel,
        out_shape=jax.ShapeDtypeStruct((rows, got.shape[1]), got.dtype),
        in_specs=[ANY],
        out_specs=ANY,
        scratch_shapes=[pltpu.SemaphoreType.DMA((1,))],
        compiler_params=params(8),
        name="widen",
    )(got)


def follow(pairs, count):
    def run(handed):
        rows = handed.shape[0]
        if count == 0:
            return handed
        got = lax.ppermute(handed[:count], "inst", pairs)
        return got if count == rows else widen(rows, got)

    return run


@functools.partial(jax.jit, static_argnums=(0, 1))
def gather(start, rows, tables, mig_req, k_cache, v_cache):
    kv_width = k_cache.shape[4]
    return pl.pallas_call(
        functools.partial(gather_kernel, start, rows),
        out_shape=jax.ShapeDtypeStruct((rows, 2 * kv_width), jnp.bfloat16),
        in_specs=[SMEM, SMEM, ANY, ANY],
        out_specs=ANY,
        scratch_shapes=[pltpu.SemaphoreType.DMA((2, rows // CHUNK))],
        compiler_params=params(8),
        name="gather",
    )(tables, mig_req, k_cache, v_cache)


def branch(offset, counts, context):
    def run(emb, attn_gain, out_gain, k_cache, v_cache, tables, lens, partner, mig_req):
        sections = lax.axis_size("section")
        tp = lax.axis_size("tp")
        pairs = [(i, i ^ offset) for i in range(lax.axis_size("inst"))]
        early = counts[0] if len(counts) > 1 else -(-context // (3 * CHUNK)) * CHUNK
        rest = context - early
        handed = gather(0, early, tables, mig_req, k_cache, v_cache)
        first = lax.ppermute(handed, "inst", pairs)
        handed = gather(early, rest, tables, mig_req, k_cache, v_cache)
        if len(counts) == 1:
            later = lax.ppermute(handed, "inst", pairs)

        hidden, prior = emb, ()
        for phase in range(sections):
            if phase > 0:
                hidden = lax.ppermute(prior[0], "section", [(phase - 1, phase)])[0]
            others = tuple(
                lax.ppermute(hidden, "tp", [(i, (i + by) % tp) for i in range(tp)])
                for by in range(1, tp)
            )
            prior = tuple(
                layer(
                    phase, tables, lens, mig_req, hidden, others, attn_gain, out_gain,
                    k_cache, v_cache, prior,
                )
            )
        fresh = lax.ppermute(prior[1], "inst", pairs)
        if len(counts) > 1:
            handed, _ = lax.optimization_barrier((handed, prior[1]))
            later = lax.switch(
                pick(tuple(counts), lens, mig_req, partner),
                [follow(pairs, count - early) for count in counts],
                handed,
            )
        arrived = place(context, lens, mig_req, partner, first, later, fresh)
        return (prior[0], arrived[0], arrived[1])

    return run


def local(emb, attn_gain, out_gain, k_cache, v_cache, tables, lens, partner, mig_req):
    instances, sections = lax.axis_size("inst"), lax.axis_size("section")
    context = tables.shape[2] * k_cache.shape[3]
    branches = [
        branch(offset, row_counts(offset, instances, sections, context), context)
        for offset in range(1, instances)
    ]
    return lax.switch(
        partner[0] - 1, branches, emb, attn_gain, out_gain, k_cache, v_cache, tables, lens,
        partner, mig_req,
    )


def solution(mesh):
    return jax.shard_map(
        local,
        mesh=mesh,
        in_specs=(
            P(None, ("groups", "inst"), "tp"),
            P("section", "tp"),
            P("section", "tp"),
            P(("groups", "inst"), "section", None, None, "tp"),
            P(("groups", "inst"), "section", None, None, "tp"),
            P(("groups", "inst"), None, None),
            P("groups", None),
            P(),
            P("groups"),
        ),
        out_specs=(
            P("section", None, ("groups", "inst"), "tp"),
            P(("groups", "inst"), "section", None, "tp"),
            P(("groups", "inst"), "section", None, "tp"),
        ),
        check_vma=False,
    )
```
